32 devices in a mesh: hi: 8 (over z, core), lo: 4 (over y, x).
Axes of the slice: x: 2, y: 2, z: 4, core: 2. Of those that a mesh axis runs over, the one named last changes fastest.
Arguments:
- amplitudes: float32 [2, 1048576], P(None, ('hi', 'lo')), may hold values from -6 to 6
- gate_mats: float32 [5, 2, 128, 128], replicated, may hold values from -0.375 to 0.375
- dev_gate: float32 [2, 2, 2], replicated, may hold values from -3 to 3
- qubit_order: int32 [15], replicated, may hold values from 0 to 14, each once
Outputs:
- final_state: float32 [2, 1048576], P(None, ('hi', 'lo'))
The draws below stay inside these ranges and needn't reach their ends.
Inputs may be any that keep to these rules, and one draw needn't show every extreme that they name: `qubit_order`: each of the 15 positions appears exactly once.
All inputs are finite; a program needn't handle non-finite values.
Results may differ from the reference program's by a relative error of at most 0.000068.
Values sent between devices are 32-bit elements; how exact they have to be, the bound alone decides.
No kernel may reach another device: no remote copies, remote signals or barrier semaphores. Data moves between devices by JAX's collectives and lax.ppermute only.
A program may use at most 128 MiB of HBM per device.

```python
import jax
import jax.numpy as jnp
from jax import lax

LOCAL_BITS = 15
GATES = 5
AMP_DEV = 32768
GATE_DIM = 128
AMPS = 1048576
N_HI = 8
N_LO = 4


def shard_levels(stream_key, extent, split, low, largest):
    gain = 1.0
    for axis_at, shards_of in split:
        draws = jax.random.uniform(jax.random.fold_in(jax.random.fold_in(stream_key, 6), axis_at), (shards_of,), jnp.float32, low / len(split), largest / len(split))
        gain = gain * jnp.repeat(jnp.exp(draws), extent[axis_at] // shards_of).reshape((-1,) + (1,) * (len(extent) - 1 - axis_at))
    return gain


def bell_draw(rng, shape, scale, reach, shards=(), kind=jnp.bfloat16):
    factor_of = shard_levels(rng, shape, shards, -0.22, 0.18) if shards else 1.0
    result = jax.random.normal(rng, shape, jnp.float32) * scale * factor_of
    return jnp.minimum(jnp.maximum(result, -reach), reach).astype(kind)


def setup_inputs(seed: int = 0) -> dict:
    splits = jax.random.split(jax.random.key(seed), 5)
    amplitudes = bell_draw(splits[0], (2, AMPS), 1.0, 6.0, ((1, 32),), jnp.float32)
    gate_mats = bell_draw(splits[1], (GATES, 2, GATE_DIM, GATE_DIM), (2 * GATE_DIM) ** -0.5, 0.375, (), jnp.float32)
    dev_gate = bell_draw(splits[2], (2, 2, 2), 4 ** -0.5, 3.0, (), jnp.float32)
    qubit_order = jax.random.permutation(splits[3], LOCAL_BITS).astype(jnp.int32)
    return {"amplitudes": amplitudes, "gate_mats": gate_mats, "dev_gate": dev_gate, "qubit_order": qubit_order}


def apply_matrix(matrix, values, pattern):
    mix_rr = jnp.einsum(pattern, matrix[0], values[0], precision=lax.Precision.HIGHEST)
    mix_ii = jnp.einsum(pattern, matrix[1], values[1], precision=lax.Precision.HIGHEST)
    mix_ri = jnp.einsum(pattern, matrix[0], values[1], precision=lax.Precision.HIGHEST)
    mix_ir = jnp.einsum(pattern, matrix[1], values[0], precision=lax.Precision.HIGHEST)
    return jnp.stack([mix_rr - mix_ii, mix_ri + mix_ir])


def low_gate(matrix, values):
    gate_width = matrix.shape[-1]
    shaped = values.reshape(2, -1, gate_width)
    return apply_matrix(matrix, shaped, "ab,mb->ma").reshape(values.shape)


def high_gate(matrix, values):
    gate_width = matrix.shape[-1]
    shaped = values.reshape(2, -1, gate_width, AMP_DEV // gate_width)
    return apply_matrix(matrix, shaped, "ab,cbm->cam").reshape(values.shape)


def mix_pair(dev_gate, row_index, lower_pair, upper_pair):
    coef_0r = dev_gate[0, row_index, 0]
    coef_0i = dev_gate[1, row_index, 0]
    coef_1r = dev_gate[0, row_index, 1]
    coef_1i = dev_gate[1, row_index, 1]
    real_part = (coef_0r * lower_pair[0] - coef_0i * lower_pair[1]) + (coef_1r * upper_pair[0] - coef_1i * upper_pair[1])
    imag_part = (coef_0r * lower_pair[1] + coef_0i * lower_pair[0]) + (coef_1r * upper_pair[1] + coef_1i * upper_pair[0])
    return jnp.stack([real_part, imag_part])


def source_table(qubit_order, amp_count):
    positions = jnp.arange(amp_count, dtype=jnp.int32)
    source = jnp.zeros((amp_count,), jnp.int32)
    for position in range(qubit_order.shape[0]):
        source = source + jnp.left_shift(jnp.right_shift(positions, position) & 1, qubit_order[position])
    return source


def reference(amplitudes, gate_mats, dev_gate, qubit_order):
    halves = amplitudes.reshape(2, 2, -1)
    lower_pair = halves[:, 0]
    upper_pair = halves[:, 1]
    state_now = jnp.stack([mix_pair(dev_gate, 0, lower_pair, upper_pair), mix_pair(dev_gate, 1, lower_pair, upper_pair)], axis=1).reshape(2, -1)
    state_now = high_gate(gate_mats[0], state_now)
    state_now = low_gate(gate_mats[1], state_now)
    source = source_table(qubit_order, AMP_DEV)
    state_now = jnp.take(state_now.reshape(2, N_HI * N_LO, AMP_DEV), source, axis=2).reshape(2, -1)
    state_now = state_now.reshape(2, N_HI, N_LO, N_LO, AMP_DEV // N_LO).swapaxes(2, 3).reshape(2, -1)
    state_now = high_gate(gate_mats[2], state_now)
    state_now = low_gate(gate_mats[3], state_now)
    return high_gate(gate_mats[4], state_now)
```

```python
import functools

import jax
import jax.numpy as jnp
from jax import lax
from jax.experimental import pallas as pl
from jax.experimental.pallas import tpu as pltpu
from jax.sharding import PartitionSpec as P

WIDTH = 128
LANE_BITS = 7
ROW_BITS = 8
F32, BF16 = jnp.float32, jnp.bfloat16


def halves(value):
    high = value.astype(BF16)
    return high, (value - high.astype(F32)).astype(BF16)


def dot(left, right, transposed=False):
    return lax.dot_general(
        left, right, (((1,), (1 if transposed else 0,)), ((), ())), preferred_element_type=F32
    )


def dot3(left, right, transposed=False):
    (lh, ll), (rh, rl) = left, right
    return dot(lh, rl, transposed) + dot(ll, rh, transposed) + dot(lh, rh, transposed)


def block_matrix(real, imag):
    return jnp.concatenate(
        [jnp.concatenate([real, -imag], axis=1), jnp.concatenate([imag, real], axis=1)], axis=0
    )


def new_positions(lo_bits):
    kept = LANE_BITS - lo_bits
    return [8 + r for r in range(kept)] + [7] + [8 + r for r in range(kept, LANE_BITS)]


def plan_of(order, lo_bits):
    one, zero = jnp.int32(1), jnp.int32(0)
    middle = LANE_BITS - lo_bits
    row_of_lane = [l if l < middle else l + 1 for l in range(LANE_BITS)]
    wanted = [order[k] for k in new_positions(lo_bits)]
    crosses = [jnp.where(w < LANE_BITS, one, zero) for w in wanted]
    crosses_middle = crosses[middle]
    used, before = [], zero
    spare = zero
    for l in range(LANE_BITS):
        free = (one - crosses[row_of_lane[l]]) * crosses_middle * jnp.where(before == 0, one, zero)
        spare = spare + free * l
        used.append(crosses[row_of_lane[l]] + free)
        before = before + free
    key_lane, moved, stayed = [], zero, zero
    for l in range(LANE_BITS):
        key_lane.append(jnp.where(used[l] == 1, moved + 16, stayed))
        moved, stayed = moved + used[l], stayed + (one - used[l])
    key_new, moved, stayed = [], zero, zero
    for k in range(LANE_BITS):
        from_row = jnp.where(order[k] >= LANE_BITS, one, zero)
        key_new.append(jnp.where(from_row == 1, moved + 16, stayed))
        moved, stayed = moved + from_row, stayed + (one - from_row)
    match = []
    for l in range(LANE_BITS):
        total = zero
        for k in range(LANE_BITS):
            total = total + jnp.where(key_lane[l] == key_new[k], order[k] + 16 * k, zero)
        match.append(total)
    new_in_lane = [m >> 4 for m in match]
    lane_before, row_before = [], [None] * ROW_BITS
    middle_before = zero
    for l in range(LANE_BITS):
        r = row_of_lane[l]
        old = match[l] & 15
        at_spare = crosses_middle * jnp.where(spare == l, one, zero)
        lane_before.append(jnp.where(crosses[r] == 1, wanted[r], jnp.where(at_spare == 1, wanted[middle], old)))
        row_before[r] = jnp.where(crosses[r] == 1, old, wanted[r]) & 7
        middle_before = middle_before + at_spare * old
    row_before[middle] = jnp.where(crosses_middle == 1, middle_before, wanted[middle]) & 7
    return crosses, spare, row_before, lane_before, new_in_lane


def moved_bits(index, sources, targets):
    total = jnp.zeros_like(index)
    for source, target in zip(sources, targets, strict=True):
        total = total | (((index >> source) & 1) << target)
    return total


def one_hot(count, index):
    rows = lax.broadcasted_iota(jnp.int32, (count, index.shape[1]), 0)
    return jnp.where(rows == index, 1.0, 0.0).astype(F32).astype(BF16)


def bit_exchange(low, high, lane, crosses, lane_bit, shift):
    up = ((lane >> lane_bit) & 1) * crosses
    down = (1 - ((lane >> lane_bit) & 1)) * crosses
    return (
        jnp.where(up == 1, pltpu.roll(high, shift, 1), low),
        jnp.where(down == 1, pltpu.roll(low, WIDTH - shift, 1), high),
    )


def first_kernel(lo_bits, order_ref, x_ref, gates_ref, *refs):
    outs, (work, blocks) = refs[:-2], refs[-2:]
    parts = 1 << lo_bits
    order = [order_ref[k] for k in range(LANE_BITS + ROW_BITS)]
    crosses, spare, row_before, lane_before, _ = plan_of(order, lo_bits)
    middle = LANE_BITS - lo_bits
    pieces = [[x_ref[pl.ds(m * 2 + c, WIDTH, stride=4), :] for m in range(2)] for c in range(2)]
    state = jnp.concatenate([jnp.concatenate(row, axis=1) for row in pieces], axis=0)
    real, imag = halves(gates_ref[0, 0]), halves(gates_ref[0, 1])
    matrix = [block_matrix(real[i], imag[i]) for i in range(2)]
    state = dot3(matrix, halves(state))
    state = jnp.concatenate(
        [
            jnp.concatenate([state[c * WIDTH : (c + 1) * WIDTH, m * WIDTH : (m + 1) * WIDTH] for c in range(2)], axis=1)
            for m in range(2)
        ],
        axis=0,
    )
    index = lax.broadcasted_iota(jnp.int32, (1, 2 * WIDTH), 1)
    rows = one_hot(2 * WIDTH, moved_bits(index, row_before, range(ROW_BITS)))
    state = [dot(rows, half).astype(BF16) for half in halves(state)]
    index = lax.broadcasted_iota(jnp.int32, (1, WIDTH), 1)
    lanes = one_hot(WIDTH, moved_bits(index, lane_before, range(LANE_BITS)))
    real, imag = halves(gates_ref[1, 0]), halves(gates_ref[1, 1])
    matrix = [
        block_matrix(dot(lanes, real[i]).astype(BF16), dot(lanes, imag[i]).astype(BF16)) for i in range(2)
    ]
    state = dot3(state, matrix, transposed=True)
    for c in range(2):
        work[c] = state[:, c * WIDTH : (c + 1) * WIDTH]
    lane = lax.broadcasted_iota(jnp.int32, (8, WIDTH), 1)

    def exchange(values, row_bit, bit):
        if row_bit == middle:
            lane_bit, shift = spare, jnp.left_shift(jnp.int32(1), spare)
        else:
            lane_bit = row_bit if row_bit < middle else row_bit - 1
            shift = 1 << lane_bit
        for i in range(len(values)):
            if not i >> bit & 1:
                j = i | 1 << bit
                values[i], values[j] = bit_exchange(values[i], values[j], lane, crosses[row_bit], lane_bit, shift)

    for c in range(2):
        for group in range(4):
            places = [pl.ds(group * 64 + o, 8, stride=8) for o in range(8)]
            values = [work[c, place, :] for place in places]
            for row_bit in range(3):
                exchange(values, row_bit, row_bit)
            for place, value in zip(places, values, strict=True):
                work[c, place, :] = value
    me = lax.axis_index("lo")
    kept = WIDTH // parts
    for c in range(2):
        values = [work[c, pl.ds(8 * v, 8), :] for v in range(32)]
        for row_bit in range(3, ROW_BITS):
            exchange(values, row_bit, row_bit - 3)
        each = 32 // parts
        for part in range(parts):
            step = jnp.bitwise_xor(me, part)
            for v in range(each):
                m, h = divmod(8 * v, kept)
                blocks[step, c, m, pl.ds(h, 8), :] = values[part * each + v]
    at = 0
    for out in outs:
        out[...] = blocks[at : at + out.shape[0]]
        at += out.shape[0]


def mixed(coefs, own, other):
    own_r, own_i, other_r, other_i = coefs
    return (
        own_r * own[0] - own_i * own[1] + (other_r * other[0] - other_i * other[1]),
        own_r * own[1] + own_i * own[0] + (other_r * other[1] + other_i * other[0]),
    )


def coefs_of(gate_ref, side):
    other = 1 - side
    return gate_ref[0, side, side], gate_ref[1, side, side], gate_ref[0, side, other], gate_ref[1, side, other]


def side_of():
    return jnp.right_shift(lax.axis_index("hi"), lax.axis_size("hi").bit_length() - 2) & 1


def mix_kernel(gate_ref, own_ref, other_ref, out_ref):
    coefs = coefs_of(gate_ref, side_of())
    for b in range(own_ref.shape[0]):
        out_ref[b, 0], out_ref[b, 1] = mixed(coefs, own_ref.at[b], other_ref.at[b])


def weights_kernel(lo_bits, order_ref, gate2_ref, gate3_ref, gate4_ref, high_ref, low_ref):
    order = [order_ref[k] for k in range(LANE_BITS + ROW_BITS)]
    new_in_lane = plan_of(order, lo_bits)[4]
    index = lax.broadcasted_iota(jnp.int32, (1, WIDTH), 1)
    lanes = one_hot(WIDTH, moved_bits(index, range(LANE_BITS), new_in_lane))
    for g, ref in enumerate((gate2_ref, gate3_ref, gate4_ref)):
        real, imag = halves(ref[0, 0]), halves(ref[0, 1])
        for i, out in enumerate((high_ref, low_ref)):
            parts = real[i], imag[i]
            if g == 1:
                parts = [dot(part, lanes).astype(BF16) for part in parts]
            out[g] = block_matrix(*parts)


def last_kernel(groups, gate_ref, high_ref, low_ref, *refs):
    ins, (out_ref, state_ref) = refs[:-2], refs[-2:]
    me = lax.axis_index("lo")
    coefs = coefs_of(gate_ref, side_of())
    step = 0
    for kind, count in groups:
        if kind == "pair":
            own, other, ins = ins[0], ins[1], ins[2:]
        else:
            own, ins = ins[0], ins[1:]
        for b in range(count):
            kept = own.shape[3]
            source = pl.multiple_of(jnp.bitwise_xor(me, step) * kept, 8)
            parts = mixed(coefs, own.at[b], other.at[b]) if kind == "pair" else (own[b, 0], own[b, 1])
            for c in range(2):
                for m in range(2):
                    state_ref[c, m, pl.ds(source, kept), :] = parts[c][m]
            step += 1
    matrix = [(high_ref[g], low_ref[g]) for g in range(3)]
    state = jnp.concatenate(
        [jnp.concatenate([state_ref[c, m] for m in range(2)], axis=1) for c in range(2)], axis=0
    )

    def turned(value):
        return jnp.concatenate(
            [
                jnp.concatenate([value[i * WIDTH : (i + 1) * WIDTH, j * WIDTH : (j + 1) * WIDTH] for i in range(2)], axis=1)
                for j in range(2)
            ],
            axis=0,
        )

    state = dot3(matrix[0], halves(state))
    state = dot3(halves(turned(state)), matrix[1], transposed=True)
    state = dot3(matrix[2], halves(turned(state)))
    for c in range(2):
        for m in range(2):
            out_ref[pl.ds(m * 2 + c, WIDTH, stride=4), :] = state[c * WIDTH : (c + 1) * WIDTH, m * WIDTH : (m + 1) * WIDTH]


def swapped(block, axis, distance):
    count = lax.axis_size(axis)
    return lax.ppermute(block, axis, [(i, i ^ distance) for i in range(count)])


SMEM = pl.BlockSpec(memory_space=pltpu.SMEM)
VMEM = pl.BlockSpec(memory_space=pltpu.VMEM)


def on_device(amplitudes, gate_mats, dev_gate, qubit_order):
    parts = lax.axis_size("lo")
    lo_bits = parts.bit_length() - 1
    top = lax.axis_size("hi") // 2
    kept = WIDTH // parts
    rows = amplitudes.reshape(2, 256, WIDTH).transpose(1, 0, 2).reshape(512, WIDTH)

    def block(count):
        return jax.ShapeDtypeStruct((count, 2, 2, kept, WIDTH), F32)

    def gate_spec(g, count):
        return pl.BlockSpec((count, 2, WIDTH, WIDTH), lambda i: (g, 0, 0, 0))

    near = parts // 2
    first = pl.pallas_call(
        functools.partial(first_kernel, lo_bits),
        grid=(1,),
        out_shape=[block(near)] + [block(1)] * (parts - near),
        in_specs=[SMEM, VMEM, gate_spec(0, 2)],
        out_specs=[VMEM] * (1 + parts - near),
        scratch_shapes=[
            pltpu.VMEM((2, 256, WIDTH), F32),
            pltpu.VMEM((parts, 2, 2, kept, WIDTH), F32),
        ],
        name="first_gates",
    )(qubit_order, rows, gate_mats)
    near_own, far_own = first[0], first[1:]
    near_other = swapped(near_own, "hi", top)
    far_own = [swapped(far, "lo", near + i) for i, far in enumerate(far_own)]
    far_other = [swapped(far, "hi", top) for far in far_own]
    high, low = pl.pallas_call(
        functools.partial(weights_kernel, lo_bits),
        grid=(1,),
        out_shape=[jax.ShapeDtypeStruct((3, 256, 256), BF16)] * 2,
        in_specs=[SMEM] + [gate_spec(2 + g, 1) for g in range(3)],
        out_specs=[VMEM] * 2,
        name="gate_weights",
    )(qubit_order, gate_mats, gate_mats, gate_mats)
    near_mixed = pl.pallas_call(
        mix_kernel, out_shape=block(near), in_specs=[SMEM, VMEM, VMEM], out_specs=VMEM, name="mix_pair"
    )(dev_gate, near_own, near_other)
    arrived = [near_mixed[0:1]] + [swapped(near_mixed[k : k + 1], "lo", k) for k in range(1, near)]
    operands = arrived
    groups = [("mixed", 1)] * near
    for own, other in zip(far_own, far_other, strict=True):
        operands = operands + [own, other]
        groups = groups + [("pair", 1)]
    out = pl.pallas_call(
        functools.partial(last_kernel, tuple(groups)),
        out_shape=jax.ShapeDtypeStruct((512, WIDTH), F32),
        in_specs=[SMEM] + [VMEM] * (2 + len(operands)),
        out_specs=VMEM,
        scratch_shapes=[pltpu.VMEM((2, 2, WIDTH, WIDTH), F32)],
        name="last_gates",
    )(dev_gate, high, low, *operands)
    return out.reshape(256, 2, WIDTH).transpose(1, 0, 2).reshape(2, -1)


def solution(mesh):
    return jax.shard_map(
        on_device,
        mesh=mesh,
        in_specs=(P(None, ("hi", "lo")), P(), P(), P()),
        out_specs=P(None, ("hi", "lo")),
        check_vma=False,
    )
```

```python
import functools

import jax
import jax.numpy as jnp
from jax import lax
from jax.experimental import pallas as pl
from jax.experimental.pallas import tpu as pltpu
from jax.sharding import PartitionSpec as P

WIDTH = 128
LANE_BITS = 7
ROW_BITS = 8
F32, BF16 = jnp.float32, jnp.bfloat16


def halves(value):
    high = value.astype(BF16)
    return high, (value - high.astype(F32)).astype(BF16)


def dot(left, right, transposed=False):
    return lax.dot_general(
        left, right, (((1,), (1 if transposed else 0,)), ((), ())), preferred_element_type=F32
    )


def dot3(left, right, transposed=False):
    (lh, ll), (rh, rl) = left, right
    return dot(lh, rl, transposed) + dot(ll, rh, transposed) + dot(lh, rh, transposed)


def block_matrix(real, imag):
    return jnp.concatenate(
        [jnp.concatenate([real, -imag], axis=1), jnp.concatenate([imag, real], axis=1)], axis=0
    )


def new_positions(lo_bits):
    kept = LANE_BITS - lo_bits
    return [8 + r for r in range(kept)] + [7] + [8 + r for r in range(kept, LANE_BITS)]


def plan_of(order, lo_bits):
    one, zero = jnp.int32(1), jnp.int32(0)
    middle = LANE_BITS - lo_bits
    row_of_lane = [l if l < middle else l + 1 for l in range(LANE_BITS)]
    wanted = [order[k] for k in new_positions(lo_bits)]
    crosses = [jnp.where(w < LANE_BITS, one, zero) for w in wanted]
    crosses_middle = crosses[middle]
    used, before = [], zero
    spare = zero
    for l in range(LANE_BITS):
        free = (one - crosses[row_of_lane[l]]) * crosses_middle * jnp.where(before == 0, one, zero)
        spare = spare + free * l
        used.append(crosses[row_of_lane[l]] + free)
        before = before + free
    key_lane, moved, stayed = [], zero, zero
    for l in range(LANE_BITS):
        key_lane.append(jnp.where(used[l] == 1, moved + 16, stayed))
        moved, stayed = moved + used[l], stayed + (one - used[l])
    key_new, moved, stayed = [], zero, zero
    for k in range(LANE_BITS):
        from_row = jnp.where(order[k] >= LANE_BITS, one, zero)
        key_new.append(jnp.where(from_row == 1, moved + 16, stayed))
        moved, stayed = moved + from_row, stayed + (one - from_row)
    match = []
    for l in range(LANE_BITS):
        total = zero
        for k in range(LANE_BITS):
            total = total + jnp.where(key_lane[l] == key_new[k], order[k] + 16 * k, zero)
        match.append(total)
    new_in_lane = [m >> 4 for m in match]
    lane_before, row_before = [], [None] * ROW_BITS
    middle_before = zero
    for l in range(LANE_BITS):
        r = row_of_lane[l]
        old = match[l] & 15
        at_spare = crosses_middle * jnp.where(spare == l, one, zero)
        lane_before.append(jnp.where(crosses[r] == 1, wanted[r], jnp.where(at_spare == 1, wanted[middle], old)))
        row_before[r] = jnp.where(crosses[r] == 1, old, wanted[r]) & 7
        middle_before = middle_before + at_spare * old
    row_before[middle] = jnp.where(crosses_middle == 1, middle_before, wanted[middle]) & 7
    return crosses, spare, row_before, lane_before, new_in_lane


def moved_bits(index, sources, targets):
    total = jnp.zeros_like(index)
    for source, target in zip(sources, targets, strict=True):
        total = total | (((index >> source) & 1) << target)
    return total


def one_hot(count, index):
    rows = lax.broadcasted_iota(jnp.int32, (count, index.shape[1]), 0)
    return jnp.where(rows == index, 1.0, 0.0).astype(F32).astype(BF16)


def bit_exchange(low, high, lane, crosses, lane_bit, shift):
    up = ((lane >> lane_bit) & 1) * crosses
    down = (1 - ((lane >> lane_bit) & 1)) * crosses
    return (
        jnp.where(up == 1, pltpu.roll(high, shift, 1), low),
        jnp.where(down == 1, pltpu.roll(low, WIDTH - shift, 1), high),
    )


def first_kernel(lo_bits, order_hbm, gate_hbm, x_hbm, gates_hbm, *refs):
    outs, (order_ref, gate_ref, x_ref, gates_ref, work, blocks, sems) = refs[:-7], refs[-7:]
    outs, (coefs_out, lanes_out) = outs[:-2], outs[-2:]
    parts = 1 << lo_bits
    fetches = [
        pltpu.make_async_copy(order_hbm, order_ref, sems.at[0]),
        pltpu.make_async_copy(gates_hbm.at[pl.ds(0, 2)], gates_ref, sems.at[1]),
        pltpu.make_async_copy(x_hbm, x_ref, sems.at[2]),
        pltpu.make_async_copy(gate_hbm, gate_ref, sems.at[3]),
    ]
    for fetch in fetches:
        fetch.start()
    fetches[0].wait()
    order = [order_ref[k] for k in range(LANE_BITS + ROW_BITS)]
    crosses, spare, row_before, lane_before, new_in_lane = plan_of(order, lo_bits)
    middle = LANE_BITS - lo_bits
    index = lax.broadcasted_iota(jnp.int32, (1, 2 * WIDTH), 1)
    rows = one_hot(2 * WIDTH, moved_bits(index, row_before, range(ROW_BITS)))
    index = lax.broadcasted_iota(jnp.int32, (1, WIDTH), 1)
    lanes = one_hot(WIDTH, moved_bits(index, lane_before, range(LANE_BITS)))
    lanes_out[...] = jnp.broadcast_to(moved_bits(index, range(LANE_BITS), new_in_lane), lanes_out.shape)
    fetches[1].wait()
    real, imag = halves(gates_ref[0, 0]), halves(gates_ref[0, 1])
    matrix0 = [block_matrix(real[i], imag[i]) for i in range(2)]
    real, imag = halves(gates_ref[1, 0]), halves(gates_ref[1, 1])
    matrix1 = [
        block_matrix(dot(lanes, real[i]).astype(BF16), dot(lanes, imag[i]).astype(BF16)) for i in range(2)
    ]
    fetches[2].wait()
    pieces = [[x_ref[pl.ds(m * 2 + c, WIDTH, stride=4), :] for m in range(2)] for c in range(2)]
    state = jnp.concatenate([jnp.concatenate(row, axis=1) for row in pieces], axis=0)
    state = dot3(matrix0, halves(state))
    state = [dot(rows, half).astype(BF16) for half in halves(turned(state))]
    state = dot3(state, matrix1, transposed=True)
    for c in range(2):
        work[c] = state[:, c * WIDTH : (c + 1) * WIDTH]
    lane = lax.broadcasted_iota(jnp.int32, (8, WIDTH), 1)

    def exchange(values, row_bit, bit):
        if row_bit == middle:
            lane_bit, shift = spare, jnp.left_shift(jnp.int32(1), spare)
        else:
            lane_bit = row_bit if row_bit < middle else row_bit - 1
            shift = 1 << lane_bit
        for i in range(len(values)):
            if not i >> bit & 1:
                j = i | 1 << bit
                values[i], values[j] = bit_exchange(values[i], values[j], lane, crosses[row_bit], lane_bit, shift)

    for c in range(2):
        for group in range(4):
            places = [pl.ds(group * 64 + o, 8, stride=8) for o in range(8)]
            values = [work[c, place, :] for place in places]
            for row_bit in range(3):
                exchange(values, row_bit, row_bit)
            for place, value in zip(places, values, strict=True):
                work[c, place, :] = value
    me = lax.axis_index("lo")
    kept = WIDTH // parts
    for c in range(2):
        values = [work[c, pl.ds(8 * v, 8), :] for v in range(32)]
        for row_bit in range(3, ROW_BITS):
            exchange(values, row_bit, row_bit - 3)
        each = 32 // parts
        for part in range(parts):
            step = jnp.bitwise_xor(me, part)
            for v in range(each):
                m, h = divmod(8 * v, kept)
                blocks[step, c, m, pl.ds(h, 8), :] = values[part * each + v]
    near = outs[0].shape[0]
    outs[0][...] = blocks[:near]
    for step, out in enumerate(outs[1:]):
        out[...] = blocks[near + step]
    fetches[3].wait()
    side = jnp.right_shift(lax.axis_index("hi"), lax.axis_size("hi").bit_length() - 2) & 1
    for other in range(2):
        for c in range(2):
            coefs_out[2 * other + c] = jnp.full((8, WIDTH), gate_ref[c, side, side ^ other])


def turned(value):
    return jnp.concatenate(
        [
            jnp.concatenate([value[i * WIDTH : (i + 1) * WIDTH, j * WIDTH : (j + 1) * WIDTH] for i in range(2)], axis=1)
            for j in range(2)
        ],
        axis=0,
    )


def mixed(coefs_ref, own, other, m):
    rows = own.shape[-2]
    own_r, own_i, other_r, other_i = [jnp.concatenate([coefs_ref[i]] * (rows // 8), axis=0) for i in range(4)]
    return (
        own_r * own[0, m] - own_i * own[1, m] + (other_r * other[0, m] - other_i * other[1, m]),
        own_r * own[1, m] + own_i * own[0, m] + (other_r * other[1, m] + other_i * other[0, m]),
    )


def mix_kernel(coefs_ref, own_ref, other_ref, *outs):
    for k, out_ref in enumerate(outs):
        for m in range(2):
            out_ref[0, m], out_ref[1, m] = mixed(coefs_ref, own_ref.at[k + 1], other_ref.at[k + 1], m)


def weights_kernel(lanes_ref, gates_hbm, high_ref, low_ref, gates_ref, sems):
    fetches = [pltpu.make_async_copy(gates_hbm.at[2 + g], gates_ref.at[g], sems.at[g]) for g in range(3)]
    for fetch in fetches:
        fetch.start()
    lanes = one_hot(WIDTH, lanes_ref[0:1])
    for g, fetch in enumerate(fetches):
        fetch.wait()
        real, imag = halves(gates_ref[g, 0]), halves(gates_ref[g, 1])
        for i, out in enumerate((high_ref, low_ref)):
            parts = real[i], imag[i]
            if g == 1:
                parts = [dot(part, lanes).astype(BF16) for part in parts]
            out[g] = block_matrix(*parts)


def last_kernel(pairs, coefs_ref, high_ref, low_ref, *refs):
    ins, (out_hbm, state_ref, out_ref, sems) = refs[:-4], refs[-4:]
    ins = (ins[0].at[0], ins[1].at[0]) + ins[2:]
    me = lax.axis_index("lo")
    for step, pair in enumerate(pairs):
        own, ins = ins[0], ins[1:]
        kept = own.shape[-2]
        source = pl.multiple_of(jnp.bitwise_xor(me, step) * kept, 8)
        if pair:
            other, ins = ins[0], ins[1:]
        for m in range(2):
            values = mixed(coefs_ref, own, other, m) if pair else (own[0, m], own[1, m])
            for c in range(2):
                state_ref[c, m, pl.ds(source, kept), :] = values[c]
    state = jnp.concatenate(
        [jnp.concatenate([state_ref[c, m] for m in range(2)], axis=1) for c in range(2)], axis=0
    )
    state = dot3((high_ref[0], low_ref[0]), halves(state))
    state = dot3(halves(turned(state)), (high_ref[1], low_ref[1]), transposed=True)
    state = halves(turned(state))
    sends = []
    half = WIDTH // 2
    for i in range(2):
        matrix = [
            jnp.concatenate([ref[2, c * WIDTH + i * half : c * WIDTH + (i + 1) * half] for c in range(2)], axis=0)
            for ref in (high_ref, low_ref)
        ]
        result = dot3(matrix, state)
        for c in range(2):
            for m in range(2):
                out_ref[pl.ds(i * 256 + m * 2 + c, half, stride=4), :] = result[
                    c * half : (c + 1) * half, m * WIDTH : (m + 1) * WIDTH
                ]
        sends.append(
            pltpu.make_async_copy(out_ref.at[pl.ds(i * 256, 256)], out_hbm.at[pl.ds(i * 256, 256)], sems.at[i])
        )
        sends[-1].start()
    for send in sends:
        send.wait()


def swapped(block, axis, distance):
    count = lax.axis_size(axis)
    return lax.ppermute(block, axis, [(i, i ^ distance) for i in range(count)])


PARAMS = pltpu.CompilerParams(vmem_limit_bytes=8 << 20)
HBM = pl.BlockSpec(memory_space=pltpu.HBM)
VMEM = pl.BlockSpec(memory_space=pltpu.VMEM)


def in_hbm(value):
    return pltpu.with_memory_space_constraint(value, pltpu.HBM)


def on_device(amplitudes, gate_mats, dev_gate, qubit_order):
    parts = lax.axis_size("lo")
    lo_bits = parts.bit_length() - 1
    top = lax.axis_size("hi") // 2
    kept = WIDTH // parts
    rows = amplitudes.reshape(2, 256, WIDTH).transpose(1, 0, 2).reshape(512, WIDTH)
    block = pltpu.VMEM((2, 2, kept, WIDTH), F32)
    near = parts // 2
    near_own, *far_own, coefs, lanes = pl.pallas_call(
        functools.partial(first_kernel, lo_bits),
        out_shape=[pltpu.VMEM((near, 2, 2, kept, WIDTH), F32)]
        + [block] * (parts - near)
        + [pltpu.VMEM((4, 8, WIDTH), F32), pltpu.VMEM((8, WIDTH), jnp.int32)],
        in_specs=[HBM] * 4,
        out_specs=[VMEM] * (parts - near + 3),
        scratch_shapes=[
            pltpu.SMEM((LANE_BITS + ROW_BITS,), jnp.int32),
            pltpu.SMEM((2, 2, 2), F32),
            pltpu.VMEM((512, WIDTH), F32),
            pltpu.VMEM((2, 2, WIDTH, WIDTH), F32),
            pltpu.VMEM((2, 256, WIDTH), F32),
            pltpu.VMEM((parts, 2, 2, kept, WIDTH), F32),
            pltpu.SemaphoreType.DMA((4,)),
        ],
        compiler_params=PARAMS,
        name="first_gates",
    )(in_hbm(qubit_order), in_hbm(dev_gate), in_hbm(rows), in_hbm(gate_mats))
    near_other = swapped(near_own, "hi", top)
    far_own = [swapped(far, "lo", near + i) for i, far in enumerate(far_own)]
    far_other = [swapped(far, "hi", top) for far in far_own]
    weights = pltpu.VMEM((3, 256, 256), BF16)
    high, low = pl.pallas_call(
        weights_kernel,
        out_shape=[weights] * 2,
        in_specs=[VMEM, HBM],
        out_specs=[VMEM] * 2,
        scratch_shapes=[pltpu.VMEM((3, 2, WIDTH, WIDTH), F32), pltpu.SemaphoreType.DMA((3,))],
        compiler_params=PARAMS,
        name="gate_weights",
    )(lanes, in_hbm(gate_mats))
    mixes = pl.pallas_call(
        mix_kernel,
        out_shape=[block] * (near - 1),
        in_specs=[VMEM] * 3,
        out_specs=[VMEM] * (near - 1),
        compiler_params=PARAMS,
        name="mix_pair",
    )(coefs, near_own, near_other)
    operands = [near_own, near_other] + [swapped(mix, "lo", 1 + i) for i, mix in enumerate(mixes)]
    pairs = [True] + [False] * (near - 1) + [True] * (parts - near)
    for pair in zip(far_own, far_other, strict=True):
        operands += pair
    out = pl.pallas_call(
        functools.partial(last_kernel, tuple(pairs)),
        out_shape=jax.ShapeDtypeStruct((512, WIDTH), F32),
        in_specs=[VMEM] * (3 + len(operands)),
        out_specs=HBM,
        scratch_shapes=[
            pltpu.VMEM((2, 2, WIDTH, WIDTH), F32),
            pltpu.VMEM((512, WIDTH), F32),
            pltpu.SemaphoreType.DMA((2,)),
        ],
        compiler_params=PARAMS,
        name="last_gates",
    )(coefs, high, low, *operands)
    return out.reshape(256, 2, WIDTH).transpose(1, 0, 2).reshape(2, -1)


def solution(mesh):
    return jax.shard_map(
        on_device,
        mesh=mesh,
        in_specs=(P(None, ("hi", "lo")), P(), P(), P()),
        out_specs=P(None, ("hi", "lo")),
        check_vma=False,
    )
```

```python
import functools

import jax
import jax.numpy as jnp
from jax import lax
from jax.experimental import pallas as pl
from jax.experimental.pallas import tpu as pltpu
from jax.sharding import PartitionSpec as P

WIDTH = 128
LANE_BITS = 7
ROW_BITS = 8
F32, BF16 = jnp.float32, jnp.bfloat16


def halves(value):
    high = value.astype(BF16)
    return high, (value - high.astype(F32)).astype(BF16)


def dot(left, right, transposed=False):
    return lax.dot_general(
        left, right, (((1,), (1 if transposed else 0,)), ((), ())), preferred_element_type=F32
    )


def dot3(left, right, transposed=False):
    (lh, ll), (rh, rl) = left, right
    return dot(lh, rl, transposed) + dot(ll, rh, transposed) + dot(lh, rh, transposed)


def block_matrix(real, imag):
    return jnp.concatenate(
        [jnp.concatenate([real, -imag], axis=1), jnp.concatenate([imag, real], axis=1)], axis=0
    )


def new_positions(lo_bits):
    kept = LANE_BITS - lo_bits
    return [8 + r for r in range(kept)] + [7] + [8 + r for r in range(kept, LANE_BITS)]


def plan_of(order, lo_bits):
    one, zero = jnp.int32(1), jnp.int32(0)
    middle = LANE_BITS - lo_bits
    row_of_lane = [l if l < middle else l + 1 for l in range(LANE_BITS)]
    wanted = [order[k] for k in new_positions(lo_bits)]
    crosses = [jnp.where(w < LANE_BITS, one, zero) for w in wanted]
    crosses_middle = crosses[middle]
    used, before = [], zero
    spare = zero
    for l in range(LANE_BITS):
        free = (one - crosses[row_of_lane[l]]) * crosses_middle * jnp.where(before == 0, one, zero)
        spare = spare + free * l
        used.append(crosses[row_of_lane[l]] + free)
        before = before + free
    key_lane, moved, stayed = [], zero, zero
    for l in range(LANE_BITS):
        key_lane.append(jnp.where(used[l] == 1, moved + 16, stayed))
        moved, stayed = moved + used[l], stayed + (one - used[l])
    key_new, moved, stayed = [], zero, zero
    for k in range(LANE_BITS):
        from_row = jnp.where(order[k] >= LANE_BITS, one, zero)
        key_new.append(jnp.where(from_row == 1, moved + 16, stayed))
        moved, stayed = moved + from_row, stayed + (one - from_row)
    match = []
    for l in range(LANE_BITS):
        total = zero
        for k in range(LANE_BITS):
            total = total + jnp.where(key_lane[l] == key_new[k], order[k] + 16 * k, zero)
        match.append(total)
    new_in_lane = [m >> 4 for m in match]
    lane_before, row_before = [], [None] * ROW_BITS
    middle_before = zero
    for l in range(LANE_BITS):
        r = row_of_lane[l]
        old = match[l] & 15
        at_spare = crosses_middle * jnp.where(spare == l, one, zero)
        lane_before.append(jnp.where(crosses[r] == 1, wanted[r], jnp.where(at_spare == 1, wanted[middle], old)))
        row_before[r] = jnp.where(crosses[r] == 1, old, wanted[r]) & 7
        middle_before = middle_before + at_spare * old
    row_before[middle] = jnp.where(crosses_middle == 1, middle_before, wanted[middle]) & 7
    slots = [r if r < middle else r - 1 for r in range(ROW_BITS)]
    slots[middle] = spare
    return crosses, wanted, slots, row_before, lane_before, new_in_lane


def moved_bits(index, sources, targets):
    total = jnp.zeros_like(index)
    for source, target in zip(sources, targets, strict=True):
        total = total | (((index >> source) & 1) << target)
    return total


def one_hot(count, index):
    rows = lax.broadcasted_iota(jnp.int32, (count, index.shape[1]), 0)
    return jnp.where(rows == index, 1.0, 0.0).astype(F32).astype(BF16)


def crossed(values, before, after, index):
    values = list(values)

    def butterfly(masks):
        for bit, mask in enumerate(masks):
            for i in range(len(values)):
                if not i >> bit & 1:
                    low, high = values[i], values[i | 1 << bit]
                    values[i] = jnp.where(mask, high, low)
                    values[i | 1 << bit] = jnp.where(mask, low, high)

    butterfly(before)
    for i, lanes in enumerate(index):
        values[i] = jnp.take_along_axis(values[i], lanes, axis=1, mode="promise_in_bounds")
    butterfly(after)
    return values


def masks_of(lane, crosses, bits):
    return [((lane >> bit) & 1) * cross == 1 for cross, bit in zip(crosses, bits, strict=True)]


def lanes_of(lane, crosses, bits):
    moves = [cross << bit for cross, bit in zip(crosses, bits, strict=True)]
    offsets = [jnp.int32(0)]
    for move in moves:
        offsets += [offset | move for offset in offsets]
    return [jnp.bitwise_xor(lane, offset) for offset in offsets]


def first_kernel(lo_bits, order_hbm, gate_hbm, x_hbm, gates_hbm, *refs):
    outs, (order_ref, gate_ref, x_ref, gates_ref, work, sems) = refs[:-6], refs[-6:]
    outs, (coefs_out, lanes_out) = outs[:-2], outs[-2:]
    parts = 1 << lo_bits
    fetches = [
        pltpu.make_async_copy(order_hbm, order_ref, sems.at[0]),
        pltpu.make_async_copy(gates_hbm.at[pl.ds(0, 2)], gates_ref, sems.at[1]),
        pltpu.make_async_copy(x_hbm, x_ref, sems.at[2]),
        pltpu.make_async_copy(gate_hbm, gate_ref, sems.at[3]),
    ]
    for fetch in fetches:
        fetch.start()
    fetches[0].wait()
    order = [order_ref[k] for k in range(LANE_BITS + ROW_BITS)]
    crosses, wanted, slots, row_before, lane_before, new_in_lane = plan_of(order, lo_bits)
    index = lax.broadcasted_iota(jnp.int32, (1, 2 * WIDTH), 1)
    rows = one_hot(2 * WIDTH, moved_bits(index, row_before, range(ROW_BITS)))
    lane = lax.broadcasted_iota(jnp.int32, (8, WIDTH), 1)
    lanes_out[...] = moved_bits(lane, range(LANE_BITS), new_in_lane)
    old_lane = moved_bits(lane, range(LANE_BITS), lane_before)
    fetches[1].wait()
    real, imag = halves(gates_ref[0, 0]), halves(gates_ref[0, 1])
    matrix0 = [block_matrix(real[i], imag[i]) for i in range(2)]
    real, imag = halves(gates_ref[1, 0]), halves(gates_ref[1, 1])
    matrix1 = [block_matrix(real[i], imag[i]) for i in range(2)]
    fetches[2].wait()
    pieces = [[x_ref[pl.ds(m * 2 + c, WIDTH, stride=4), :] for m in range(2)] for c in range(2)]
    state = jnp.concatenate([jnp.concatenate(row, axis=1) for row in pieces], axis=0)
    state = dot3(matrix0, halves(state))
    state = [dot(rows, half).astype(BF16) for half in halves(turned(state))]
    state = dot3(state, matrix1, transposed=True)
    before, after = masks_of(lane, crosses[3:], wanted[3:]), masks_of(lane, crosses[3:], slots[3:])
    index = lanes_of(old_lane, crosses[3:], wanted[3:])
    for c in range(2):
        values = [state[8 * v : 8 * v + 8, c * WIDTH : (c + 1) * WIDTH] for v in range(32)]
        for v, value in enumerate(crossed(values, before, after, index)):
            work[c, pl.ds(8 * v, 8), :] = value
    masks = masks_of(lane, crosses[:3], slots[:3])
    index = lanes_of(lane, crosses[:3], slots[:3])
    for c in range(2):
        for group in range(4):
            places = [pl.ds(group * 64 + o, 8, stride=8) for o in range(8)]
            values = crossed([work[c, place, :] for place in places], masks, masks, index)
            for place, value in zip(places, values, strict=True):
                work[c, place, :] = value
    me = lax.axis_index("lo")
    count = 2 * WIDTH // parts
    near = outs[0].shape[0]
    for step in range(parts):
        out = outs[0].at[step] if step < near else outs[1 + step - near]
        source = pl.multiple_of(jnp.bitwise_xor(me, step) * count, 8)
        for c in range(2):
            out[c] = work[c, pl.ds(source, count), :]
    fetches[3].wait()
    side = jnp.right_shift(lax.axis_index("hi"), lax.axis_size("hi").bit_length() - 2) & 1
    for other in range(2):
        for c in range(2):
            coefs_out[2 * other + c] = jnp.full((8, WIDTH), gate_ref[c, side, side ^ other])


def turned(value):
    return jnp.concatenate(
        [
            jnp.concatenate([value[i * WIDTH : (i + 1) * WIDTH, j * WIDTH : (j + 1) * WIDTH] for i in range(2)], axis=1)
            for j in range(2)
        ],
        axis=0,
    )


def mixed(coefs_ref, own, other):
    own_r, own_i, other_r, other_i = [jnp.concatenate([coefs_ref[i]] * (own.shape[-2] // 8), axis=0) for i in range(4)]
    return (
        own_r * own[0] - own_i * own[1] + (other_r * other[0] - other_i * other[1]),
        own_r * own[1] + own_i * own[0] + (other_r * other[1] + other_i * other[0]),
    )


def mix_kernel(coefs_ref, own_ref, other_ref, *outs):
    for k, out_ref in enumerate(outs):
        out_ref[0], out_ref[1] = mixed(coefs_ref, own_ref.at[k + 1], other_ref.at[k + 1])


def weights_kernel(lo_bits, lanes_ref, gates_hbm, high_ref, low_ref, gates_ref, sems):
    fetches = [pltpu.make_async_copy(gates_hbm.at[2 + g], gates_ref.at[g], sems.at[g]) for g in range(3)]
    for fetch in fetches:
        fetch.start()
    lanes = one_hot(WIDTH, lanes_ref[0:1])
    me = lax.axis_index("lo")
    rows = one_hot(WIDTH, jnp.bitwise_xor(lax.broadcasted_iota(jnp.int32, (1, WIDTH), 1), me * (WIDTH >> lo_bits)))
    for fetch in fetches:
        fetch.wait()
    first = [[dot(part, rows).astype(BF16) for part in halves(gates_ref[0, c])] for c in range(2)]
    last = [halves(gates_ref[2, c]) for c in range(2)]
    real = halves(dot3(last[0], first[0]) - dot3(last[1], first[1]))
    imag = halves(dot3(last[0], first[1]) + dot3(last[1], first[0]))
    for i, out in enumerate((high_ref, low_ref)):
        out[0] = block_matrix(*[dot(halves(gates_ref[1, c])[i], lanes).astype(BF16) for c in range(2)])
        out[1] = block_matrix(real[i], imag[i])


def low_gate(high_ref, low_ref, values):
    state = jnp.concatenate([jnp.concatenate(value, axis=1) for value in values], axis=0)
    return dot3(halves(state), (high_ref[0], low_ref[0]), transposed=True)


def early_kernel(coefs_ref, high_ref, low_ref, near_own_ref, near_other_ref, *refs):
    ins, out_ref = refs[:-1], refs[-1]
    values = [mixed(coefs_ref, near_own_ref.at[0], near_other_ref.at[0])]
    values += [mixed(coefs_ref, own, other) for own, other in zip(ins[0::2], ins[1::2], strict=True)]
    state = low_gate(high_ref, low_ref, values)
    out_ref[...] = state


def last_kernel(near, coefs_ref, high_ref, low_ref, early_ref, own_ref, other_ref, *refs):
    ins, (out_hbm, out_ref, sems) = refs[:-3], refs[-3:]
    values = [(ref[0], ref[1]) for ref in ins] + [mixed(coefs_ref, own_ref, other_ref)]
    state = low_gate(high_ref, low_ref, values)
    count = values[0][0].shape[0]
    kept = count // 2
    blocks = [early_ref[i * count : (i + 1) * count] for i in range(early_ref.shape[0] // count)]
    late = [state[i * count : (i + 1) * count] for i in range(len(values))]
    blocks = blocks[:1] + late[:-1] + blocks[1:] + late[-1:]
    state = jnp.concatenate(
        [
            jnp.concatenate(
                [
                    jnp.concatenate([block[m * kept : (m + 1) * kept, c * WIDTH : (c + 1) * WIDTH] for block in blocks], axis=0)
                    for m in range(2)
                ],
                axis=1,
            )
            for c in range(2)
        ],
        axis=0,
    )
    state = halves(state)
    sends = []
    half = WIDTH // 2
    for i in range(2):
        matrix = [
            jnp.concatenate([ref[1, c * WIDTH + i * half : c * WIDTH + (i + 1) * half] for c in range(2)], axis=0)
            for ref in (high_ref, low_ref)
        ]
        result = dot3(matrix, state)
        for c in range(2):
            for m in range(2):
                out_ref[pl.ds(i * 256 + m * 2 + c, half, stride=4), :] = result[
                    c * half : (c + 1) * half, m * WIDTH : (m + 1) * WIDTH
                ]
        sends.append(
            pltpu.make_async_copy(out_ref.at[pl.ds(i * 256, 256)], out_hbm.at[pl.ds(i * 256, 256)], sems.at[i])
        )
        sends[-1].start()
    for send in sends:
        send.wait()


def swapped(block, axis, distance):
    count = lax.axis_size(axis)
    return lax.ppermute(block, axis, [(i, i ^ distance) for i in range(count)])


PARAMS = pltpu.CompilerParams(vmem_limit_bytes=8 << 20)
HBM = pl.BlockSpec(memory_space=pltpu.HBM)
VMEM = pl.BlockSpec(memory_space=pltpu.VMEM)


def in_hbm(value):
    return pltpu.with_memory_space_constraint(value, pltpu.HBM)


def on_device(amplitudes, gate_mats, dev_gate, qubit_order):
    parts = lax.axis_size("lo")
    lo_bits = parts.bit_length() - 1
    top = lax.axis_size("hi") // 2
    kept = WIDTH // parts
    rows = amplitudes.reshape(2, 256, WIDTH).transpose(1, 0, 2).reshape(512, WIDTH)
    block = pltpu.VMEM((2, 2 * kept, WIDTH), F32)
    near = parts // 2
    near_own, *far_own, coefs, lanes = pl.pallas_call(
        functools.partial(first_kernel, lo_bits),
        out_shape=[pltpu.VMEM((near, 2, 2 * kept, WIDTH), F32)]
        + [block] * (parts - near)
        + [pltpu.VMEM((4, 8, WIDTH), F32), pltpu.VMEM((8, WIDTH), jnp.int32)],
        in_specs=[HBM] * 4,
        out_specs=[VMEM] * (parts - near + 3),
        scratch_shapes=[
            pltpu.SMEM((LANE_BITS + ROW_BITS,), jnp.int32),
            pltpu.SMEM((2, 2, 2), F32),
            pltpu.VMEM((512, WIDTH), F32),
            pltpu.VMEM((2, 2, WIDTH, WIDTH), F32),
            pltpu.VMEM((2, 256, WIDTH), F32),
            pltpu.SemaphoreType.DMA((4,)),
        ],
        compiler_params=PARAMS,
        name="first_gates",
    )(in_hbm(qubit_order), in_hbm(dev_gate), in_hbm(rows), in_hbm(gate_mats))
    near_other = swapped(near_own, "hi", top)
    far_own = [swapped(far, "lo", near + i) for i, far in enumerate(far_own)]
    far_other = [swapped(far, "hi", top) for far in far_own]
    weights = pltpu.VMEM((2, 256, 256), BF16)
    high, low = pl.pallas_call(
        functools.partial(weights_kernel, lo_bits),
        out_shape=[weights] * 2,
        in_specs=[VMEM, HBM],
        out_specs=[VMEM] * 2,
        scratch_shapes=[pltpu.VMEM((3, 2, WIDTH, WIDTH), F32), pltpu.SemaphoreType.DMA((3,))],
        compiler_params=PARAMS,
        name="gate_weights",
    )(lanes, in_hbm(gate_mats))
    mixes = pl.pallas_call(
        mix_kernel,
        out_shape=[block] * (near - 1),
        in_specs=[VMEM] * 3,
        out_specs=[VMEM] * (near - 1),
        compiler_params=PARAMS,
        name="mix_pair",
    )(coefs, near_own, near_other)
    mixes = [swapped(mix, "lo", 1 + i) for i, mix in enumerate(mixes)]
    pairs = [value for pair in zip(far_own[:-1], far_other[:-1], strict=True) for value in pair]
    early = pl.pallas_call(
        early_kernel,
        out_shape=pltpu.VMEM(((parts - near) * 2 * kept, 2 * WIDTH), F32),
        in_specs=[VMEM] * (5 + len(pairs)),
        out_specs=VMEM,
        compiler_params=PARAMS,
        name="early_gate",
    )(coefs, high, low, near_own, near_other, *pairs)
    out = pl.pallas_call(
        functools.partial(last_kernel, near),
        out_shape=jax.ShapeDtypeStruct((512, WIDTH), F32),
        in_specs=[VMEM] * (6 + len(mixes)),
        out_specs=HBM,
        scratch_shapes=[pltpu.VMEM((512, WIDTH), F32), pltpu.SemaphoreType.DMA((2,))],
        compiler_params=PARAMS,
        name="last_gates",
    )(coefs, high, low, early, far_own[-1], far_other[-1], *mixes)
    return out.reshape(256, 2, WIDTH).transpose(1, 0, 2).reshape(2, -1)


def solution(mesh):
    return jax.shard_map(
        on_device,
        mesh=mesh,
        in_specs=(P(None, ("hi", "lo")), P(), P(), P()),
        out_specs=P(None, ("hi", "lo")),
        check_vma=False,
    )
```

```python
import functools

import jax
import jax.numpy as jnp
from jax import lax
from jax.experimental import pallas as pl
from jax.experimental.pallas import tpu as pltpu
from jax.sharding import PartitionSpec as P

WIDTH = 128
LANE_BITS = 7
ROW_BITS = 8
F32, BF16 = jnp.float32, jnp.bfloat16


def halves(value):
    high = value.astype(BF16)
    return high, (value - high.astype(F32)).astype(BF16)


def dot(left, right, transposed=False):
    return lax.dot_general(
        left, right, (((1,), (1 if transposed else 0,)), ((), ())), preferred_element_type=F32
    )


def dot3(left, right, transposed=False):
    (lh, ll), (rh, rl) = left, right
    return dot(lh, rl, transposed) + dot(ll, rh, transposed) + dot(lh, rh, transposed)


def block_matrix(real, imag):
    return jnp.concatenate(
        [jnp.concatenate([real, -imag], axis=1), jnp.concatenate([imag, real], axis=1)], axis=0
    )


def new_positions(lo_bits):
    kept = LANE_BITS - lo_bits
    return [8 + r for r in range(kept)] + [7] + [8 + r for r in range(kept, LANE_BITS)]


def plan_of(order, lo_bits):
    one, zero = jnp.int32(1), jnp.int32(0)
    middle = LANE_BITS - lo_bits
    row_of_lane = [l if l < middle else l + 1 for l in range(LANE_BITS)]
    wanted = [order[k] for k in new_positions(lo_bits)]
    crosses = [jnp.where(w < LANE_BITS, one, zero) for w in wanted]
    crosses_middle = crosses[middle]
    used, before = [], zero
    spare = zero
    for l in range(LANE_BITS):
        free = (one - crosses[row_of_lane[l]]) * crosses_middle * jnp.where(before == 0, one, zero)
        spare = spare + free * l
        used.append(crosses[row_of_lane[l]] + free)
        before = before + free
    key_lane, moved, stayed = [], zero, zero
    for l in range(LANE_BITS):
        key_lane.append(jnp.where(used[l] == 1, moved + 16, stayed))
        moved, stayed = moved + used[l], stayed + (one - used[l])
    key_new, moved, stayed = [], zero, zero
    for k in range(LANE_BITS):
        from_row = jnp.where(order[k] >= LANE_BITS, one, zero)
        key_new.append(jnp.where(from_row == 1, moved + 16, stayed))
        moved, stayed = moved + from_row, stayed + (one - from_row)
    match = []
    for l in range(LANE_BITS):
        total = zero
        for k in range(LANE_BITS):
            total = total + jnp.where(key_lane[l] == key_new[k], order[k] + 16 * k, zero)
        match.append(total)
    new_in_lane = [m >> 4 for m in match]
    lane_before, row_before = [], [None] * ROW_BITS
    middle_before = zero
    for l in range(LANE_BITS):
        r = row_of_lane[l]
        old = match[l] & 15
        at_spare = crosses_middle * jnp.where(spare == l, one, zero)
        lane_before.append(jnp.where(crosses[r] == 1, wanted[r], jnp.where(at_spare == 1, wanted[middle], old)))
        row_before[r] = jnp.where(crosses[r] == 1, old, wanted[r]) & 7
        middle_before = middle_before + at_spare * old
    row_before[middle] = jnp.where(crosses_middle == 1, middle_before, wanted[middle]) & 7
    slots = [r if r < middle else r - 1 for r in range(ROW_BITS)]
    slots[middle] = spare
    return crosses, wanted, slots, row_before, lane_before, new_in_lane


def moved_bits(index, sources, targets):
    total = jnp.zeros_like(index)
    for source, target in zip(sources, targets, strict=True):
        total = total | (((index >> source) & 1) << target)
    return total


def one_hot(count, index):
    rows = lax.broadcasted_iota(jnp.int32, (count, index.shape[1]), 0)
    return jnp.where(rows == index, 1.0, 0.0).astype(F32).astype(BF16)


def crossed(values, before, after, index):
    values = list(values)

    def butterfly(masks):
        for bit, mask in enumerate(masks):
            for i in range(len(values)):
                if not i >> bit & 1:
                    low, high = values[i], values[i | 1 << bit]
                    values[i] = jnp.where(mask, high, low)
                    values[i | 1 << bit] = jnp.where(mask, low, high)

    butterfly(before)
    for i, lanes in enumerate(index):
        values[i] = jnp.take_along_axis(values[i], lanes, axis=1, mode="promise_in_bounds")
    butterfly(after)
    return values


def masks_of(lane, crosses, bits):
    return [((lane >> bit) & 1) * cross == 1 for cross, bit in zip(crosses, bits, strict=True)]


def lanes_of(lane, crosses, bits):
    moves = [cross << bit for cross, bit in zip(crosses, bits, strict=True)]
    offsets = [jnp.int32(0)]
    for move in moves:
        offsets += [offset | move for offset in offsets]
    return [jnp.bitwise_xor(lane, offset) for offset in offsets]


def first_kernel(lo_bits, order_hbm, gate_hbm, x_hbm, gates_hbm, *refs):
    outs, (order_ref, gate_ref, x_ref, gates_ref, work, sems) = refs[:-6], refs[-6:]
    outs, (coefs_out, lanes_out) = outs[:-2], outs[-2:]
    parts = 1 << lo_bits
    fetches = [
        pltpu.make_async_copy(order_hbm, order_ref, sems.at[0]),
        pltpu.make_async_copy(gates_hbm.at[pl.ds(0, 2)], gates_ref, sems.at[1]),
        pltpu.make_async_copy(x_hbm, x_ref, sems.at[2]),
        pltpu.make_async_copy(gate_hbm, gate_ref, sems.at[3]),
    ]
    for fetch in fetches:
        fetch.start()
    fetches[0].wait()
    order = [order_ref[k] for k in range(LANE_BITS + ROW_BITS)]
    crosses, wanted, slots, row_before, lane_before, new_in_lane = plan_of(order, lo_bits)
    index = lax.broadcasted_iota(jnp.int32, (1, 2 * WIDTH), 1)
    rows = one_hot(2 * WIDTH, moved_bits(index, row_before, range(ROW_BITS)))
    lane = lax.broadcasted_iota(jnp.int32, (8, WIDTH), 1)
    lanes_out[...] = moved_bits(lane, range(LANE_BITS), new_in_lane)
    old_lane = moved_bits(lane, range(LANE_BITS), lane_before)
    fetches[1].wait()
    real, imag = halves(gates_ref[0, 0]), halves(gates_ref[0, 1])
    matrix0 = [block_matrix(real[i], imag[i]) for i in range(2)]
    real, imag = halves(gates_ref[1, 0]), halves(gates_ref[1, 1])
    matrix1 = [block_matrix(real[i], imag[i]) for i in range(2)]
    fetches[2].wait()
    pieces = [[x_ref[pl.ds(m * 2 + c, WIDTH, stride=4), :] for m in range(2)] for c in range(2)]
    state = jnp.concatenate([jnp.concatenate(row, axis=1) for row in pieces], axis=0)
    state = dot3(matrix0, halves(state))
    state = [dot(rows, half).astype(BF16) for half in halves(turned(state))]
    state = dot3(state, matrix1, transposed=True)
    before, after = masks_of(lane, crosses[3:], wanted[3:]), masks_of(lane, crosses[3:], slots[3:])
    index = lanes_of(old_lane, crosses[3:], wanted[3:])
    for c in range(2):
        values = [state[8 * v : 8 * v + 8, c * WIDTH : (c + 1) * WIDTH] for v in range(32)]
        for v, value in enumerate(crossed(values, before, after, index)):
            work[c, pl.ds(8 * v, 8), :] = value
    masks = masks_of(lane, crosses[:3], slots[:3])
    index = lanes_of(lane, crosses[:3], slots[:3])
    for c in range(2):
        for group in range(4):
            places = [pl.ds(group * 64 + o, 8, stride=8) for o in range(8)]
            values = crossed([work[c, place, :] for place in places], masks, masks, index)
            for place, value in zip(places, values, strict=True):
                work[c, place, :] = value
    me = lax.axis_index("lo")
    count = 2 * WIDTH // parts
    near = outs[0].shape[0]
    for step in range(parts):
        out = outs[0].at[step] if step < near else outs[1 + step - near]
        source = pl.multiple_of(jnp.bitwise_xor(me, step) * count, 8)
        for c in range(2):
            out[c] = work[c, pl.ds(source, count), :]
    fetches[3].wait()
    side = jnp.right_shift(lax.axis_index("hi"), lax.axis_size("hi").bit_length() - 2) & 1
    for other in range(2):
        for c in range(2):
            coefs_out[2 * other + c] = jnp.full((8, WIDTH), gate_ref[c, side, side ^ other])


def turned(value):
    return jnp.concatenate(
        [
            jnp.concatenate([value[i * WIDTH : (i + 1) * WIDTH, j * WIDTH : (j + 1) * WIDTH] for i in range(2)], axis=1)
            for j in range(2)
        ],
        axis=0,
    )


def mixed(coefs_ref, own, other):
    own_r, own_i, other_r, other_i = [jnp.concatenate([coefs_ref[i]] * (own.shape[-2] // 8), axis=0) for i in range(4)]
    return (
        own_r * own[0] - own_i * own[1] + (other_r * other[0] - other_i * other[1]),
        own_r * own[1] + own_i * own[0] + (other_r * other[1] + other_i * other[0]),
    )


def mix_kernel(coefs_ref, own_ref, other_ref, *outs):
    for k, out_ref in enumerate(outs):
        out_ref[0], out_ref[1] = mixed(coefs_ref, own_ref.at[k + 1], other_ref.at[k + 1])


def arrival(parts):
    near = parts // 2
    return [0, *range(near, parts - 1)], [*range(1, near), parts - 1]


def weights_kernel(lo_bits, lanes_ref, gates_hbm, low_gate_ref, early_ref, late_ref, gates_ref, sems):
    fetches = [pltpu.make_async_copy(gates_hbm.at[2 + g], gates_ref.at[g], sems.at[g]) for g in range(3)]
    for fetch in fetches:
        fetch.start()
    lanes = one_hot(WIDTH, lanes_ref[0:1])
    parts = 1 << lo_bits
    kept = WIDTH // parts
    me = lax.axis_index("lo")
    index = lax.broadcasted_iota(jnp.int32, (1, WIDTH), 1)
    source = index % kept
    early, late = arrival(parts)
    for place, step in enumerate(early + late):
        source = source + jnp.where(index // kept == place, jnp.bitwise_xor(me, step) * kept, 0)
    rows = one_hot(WIDTH, source)
    for fetch in fetches:
        fetch.wait()

    def exact(left, right):
        return lax.dot_general(
            left, right, (((1,), (0,)), ((), ())), precision=lax.Precision.HIGHEST, preferred_element_type=F32
        )

    first, last = [gates_ref[0, c] for c in range(2)], [gates_ref[2, c] for c in range(2)]
    real = halves(exact(last[0], first[0]) - exact(last[1], first[1]))
    imag = halves(exact(last[0], first[1]) + exact(last[1], first[0]))
    half = len(early) * kept
    for i in range(2):
        real3, imag3 = [dot(halves(gates_ref[1, c])[i], lanes).T for c in range(2)]
        low_gate_ref[i] = block_matrix(real3, -imag3).astype(BF16)
        both = [dot(part[i], rows) for part in (real, imag)]
        early_ref[i] = block_matrix(*[part[:, :half] for part in both]).astype(BF16)
        late_ref[i] = block_matrix(*[part[:, half:] for part in both]).astype(BF16)


def low_gate(matrix_ref, values):
    state = jnp.concatenate([jnp.concatenate(value, axis=1) for value in values], axis=0)
    state = dot3(halves(state), (matrix_ref[0], matrix_ref[1]))
    count = state.shape[0] // len(values)
    kept = count // 2
    return jnp.concatenate(
        [
            jnp.concatenate(
                [
                    state[i * count + m * kept : i * count + (m + 1) * kept, c * WIDTH : (c + 1) * WIDTH]
                    for m in range(2)
                ],
                axis=1,
            )
            for c in range(2)
            for i in range(len(values))
        ],
        axis=0,
    )


def early_kernel(coefs_ref, low_gate_ref, high_gate_ref, near_own_ref, near_other_ref, *refs):
    ins, out_ref = refs[:-1], refs[-1]
    values = [mixed(coefs_ref, near_own_ref.at[0], near_other_ref.at[0])]
    values += [mixed(coefs_ref, own, other) for own, other in zip(ins[0::2], ins[1::2], strict=True)]
    out_ref[...] = dot3((high_gate_ref[0], high_gate_ref[1]), halves(low_gate(low_gate_ref, values)))


def last_kernel(coefs_ref, low_gate_ref, high_gate_ref, early_ref, own_ref, other_ref, *refs):
    ins, (out_hbm, out_ref, sems) = refs[:-3], refs[-3:]
    values = [(ref[0], ref[1]) for ref in ins] + [mixed(coefs_ref, own_ref, other_ref)]
    high, low = halves(low_gate(low_gate_ref, values))
    state = jnp.concatenate([low, high, high], axis=0)
    sends = []
    half = WIDTH // 2
    for i in range(2):
        matrix = [
            jnp.concatenate(
                [high_gate_ref[j, c * WIDTH + i * half : c * WIDTH + (i + 1) * half] for c in range(2)], axis=0
            )
            for j in (0, 1, 0)
        ]
        result = dot(jnp.concatenate(matrix, axis=1), state)
        for c in range(2):
            for m in range(2):
                at = c * WIDTH + i * half
                out_ref[pl.ds(i * 256 + m * 2 + c, half, stride=4), :] = (
                    early_ref[at : at + half, m * WIDTH : (m + 1) * WIDTH]
                    + result[c * half : (c + 1) * half, m * WIDTH : (m + 1) * WIDTH]
                )
        sends.append(
            pltpu.make_async_copy(out_ref.at[pl.ds(i * 256, 256)], out_hbm.at[pl.ds(i * 256, 256)], sems.at[i])
        )
        sends[-1].start()
    for send in sends:
        send.wait()


def swapped(block, axis, distance):
    count = lax.axis_size(axis)
    return lax.ppermute(block, axis, [(i, i ^ distance) for i in range(count)])


PARAMS = pltpu.CompilerParams(vmem_limit_bytes=8 << 20)
HBM = pl.BlockSpec(memory_space=pltpu.HBM)
VMEM = pl.BlockSpec(memory_space=pltpu.VMEM)


def in_hbm(value):
    return pltpu.with_memory_space_constraint(value, pltpu.HBM)


def on_device(amplitudes, gate_mats, dev_gate, qubit_order):
    parts = lax.axis_size("lo")
    lo_bits = parts.bit_length() - 1
    top = lax.axis_size("hi") // 2
    kept = WIDTH // parts
    rows = amplitudes.reshape(2, 256, WIDTH).transpose(1, 0, 2).reshape(512, WIDTH)
    block = pltpu.VMEM((2, 2 * kept, WIDTH), F32)
    near = parts // 2
    near_own, *far_own, coefs, lanes = pl.pallas_call(
        functools.partial(first_kernel, lo_bits),
        out_shape=[pltpu.VMEM((near, 2, 2 * kept, WIDTH), F32)]
        + [block] * (parts - near)
        + [pltpu.VMEM((4, 8, WIDTH), F32), pltpu.VMEM((8, WIDTH), jnp.int32)],
        in_specs=[HBM] * 4,
        out_specs=[VMEM] * (parts - near + 3),
        scratch_shapes=[
            pltpu.SMEM((LANE_BITS + ROW_BITS,), jnp.int32),
            pltpu.SMEM((2, 2, 2), F32),
            pltpu.VMEM((512, WIDTH), F32),
            pltpu.VMEM((2, 2, WIDTH, WIDTH), F32),
            pltpu.VMEM((2, 256, WIDTH), F32),
            pltpu.SemaphoreType.DMA((4,)),
        ],
        compiler_params=PARAMS,
        name="first_gates",
    )(in_hbm(qubit_order), in_hbm(dev_gate), in_hbm(rows), in_hbm(gate_mats))
    near_other = swapped(near_own, "hi", top)
    far_own = [swapped(far, "lo", near + i) for i, far in enumerate(far_own)]
    far_other = [swapped(far, "hi", top) for far in far_own]
    counts = [2 * kept * len(steps) for steps in arrival(parts)]
    low_weights, early_weights, late_weights = pl.pallas_call(
        functools.partial(weights_kernel, lo_bits),
        out_shape=[pltpu.VMEM((2, 256, count), BF16) for count in (256, *counts)],
        in_specs=[VMEM, HBM],
        out_specs=[VMEM] * 3,
        scratch_shapes=[pltpu.VMEM((3, 2, WIDTH, WIDTH), F32), pltpu.SemaphoreType.DMA((3,))],
        compiler_params=PARAMS,
        name="gate_weights",
    )(lanes, in_hbm(gate_mats))
    mixes = pl.pallas_call(
        mix_kernel,
        out_shape=[block] * (near - 1),
        in_specs=[VMEM] * 3,
        out_specs=[VMEM] * (near - 1),
        compiler_params=PARAMS,
        name="mix_pair",
    )(coefs, near_own, near_other)
    mixes = [swapped(mix, "lo", 1 + i) for i, mix in enumerate(mixes)]
    pairs = [value for pair in zip(far_own[:-1], far_other[:-1], strict=True) for value in pair]
    early = pl.pallas_call(
        early_kernel,
        out_shape=pltpu.VMEM((256, 256), F32),
        in_specs=[VMEM] * (5 + len(pairs)),
        out_specs=VMEM,
        compiler_params=PARAMS,
        name="early_gate",
    )(coefs, low_weights, early_weights, near_own, near_other, *pairs)
    out = pl.pallas_call(
        last_kernel,
        out_shape=jax.ShapeDtypeStruct((512, WIDTH), F32),
        in_specs=[VMEM] * (6 + len(mixes)),
        out_specs=HBM,
        scratch_shapes=[pltpu.VMEM((512, WIDTH), F32), pltpu.SemaphoreType.DMA((2,))],
        compiler_params=PARAMS,
        name="last_gates",
    )(coefs, low_weights, late_weights, early, far_own[-1], far_other[-1], *mixes)
    return out.reshape(256, 2, WIDTH).transpose(1, 0, 2).reshape(2, -1)


def solution(mesh):
    return jax.shard_map(
        on_device,
        mesh=mesh,
        in_specs=(P(None, ("hi", "lo")), P(), P(), P()),
        out_specs=P(None, ("hi", "lo")),
        check_vma=False,
    )
```

```python
import functools

import jax
import jax.numpy as jnp
from jax import lax
from jax.experimental import pallas as pl
from jax.experimental.pallas import tpu as pltpu
from jax.sharding import PartitionSpec as P

WIDTH = 128
LANE_BITS = 7
ROW_BITS = 8
F32, BF16 = jnp.float32, jnp.bfloat16


def halves(value):
    high = value.astype(BF16)
    return high, (value - high.astype(F32)).astype(BF16)


def dot(left, right, transposed=False):
    return lax.dot_general(
        left, right, (((1,), (1 if transposed else 0,)), ((), ())), preferred_element_type=F32
    )


def dot3(left, right, transposed=False):
    (lh, ll), (rh, rl) = left, right
    return dot(lh, rl, transposed) + dot(ll, rh, transposed) + dot(lh, rh, transposed)


def block_matrix(real, imag):
    return jnp.concatenate(
        [jnp.concatenate([real, -imag], axis=1), jnp.concatenate([imag, real], axis=1)], axis=0
    )


def new_positions(lo_bits):
    kept = LANE_BITS - lo_bits
    return [8 + r for r in range(kept)] + [7] + [8 + r for r in range(kept, LANE_BITS)]


def plan_of(order, lo_bits):
    one, zero = jnp.int32(1), jnp.int32(0)
    middle = LANE_BITS - lo_bits
    row_of_lane = [l if l < middle else l + 1 for l in range(LANE_BITS)]
    wanted = [order[k] for k in new_positions(lo_bits)]
    crosses = [jnp.where(w < LANE_BITS, one, zero) for w in wanted]
    crosses_middle = crosses[middle]
    used, before = [], zero
    spare = zero
    for l in range(LANE_BITS):
        free = (one - crosses[row_of_lane[l]]) * crosses_middle * jnp.where(before == 0, one, zero)
        spare = spare + free * l
        used.append(crosses[row_of_lane[l]] + free)
        before = before + free
    key_lane, moved, stayed = [], zero, zero
    for l in range(LANE_BITS):
        key_lane.append(jnp.where(used[l] == 1, moved + 16, stayed))
        moved, stayed = moved + used[l], stayed + (one - used[l])
    key_new, moved, stayed = [], zero, zero
    for k in range(LANE_BITS):
        from_row = jnp.where(order[k] >= LANE_BITS, one, zero)
        key_new.append(jnp.where(from_row == 1, moved + 16, stayed))
        moved, stayed = moved + from_row, stayed + (one - from_row)
    match = []
    for l in range(LANE_BITS):
        total = zero
        for k in range(LANE_BITS):
            total = total + jnp.where(key_lane[l] == key_new[k], order[k] + 16 * k, zero)
        match.append(total)
    new_in_lane = [m >> 4 for m in match]
    lane_before, row_before = [], [None] * ROW_BITS
    middle_before = zero
    for l in range(LANE_BITS):
        r = row_of_lane[l]
        old = match[l] & 15
        at_spare = crosses_middle * jnp.where(spare == l, one, zero)
        lane_before.append(jnp.where(crosses[r] == 1, wanted[r], jnp.where(at_spare == 1, wanted[middle], old)))
        row_before[r] = jnp.where(crosses[r] == 1, old, wanted[r]) & 7
        middle_before = middle_before + at_spare * old
    row_before[middle] = jnp.where(crosses_middle == 1, middle_before, wanted[middle]) & 7
    slots = [r if r < middle else r - 1 for r in range(ROW_BITS)]
    slots[middle] = spare
    return crosses, wanted, slots, row_before, lane_before, new_in_lane


def moved_bits(index, sources, targets):
    total = jnp.zeros_like(index)
    for source, target in zip(sources, targets, strict=True):
        total = total | (((index >> source) & 1) << target)
    return total


def one_hot(count, index):
    rows = lax.broadcasted_iota(jnp.int32, (count, index.shape[1]), 0)
    return jnp.where(rows == index, 1.0, 0.0).astype(F32).astype(BF16)


def crossed(values, before, after, index):
    values = list(values)

    def butterfly(masks):
        for bit, mask in enumerate(masks):
            for i in range(len(values)):
                if not i >> bit & 1:
                    low, high = values[i], values[i | 1 << bit]
                    values[i] = jnp.where(mask, high, low)
                    values[i | 1 << bit] = jnp.where(mask, low, high)

    butterfly(before)
    for i, lanes in enumerate(index):
        values[i] = jnp.take_along_axis(values[i], lanes, axis=1, mode="promise_in_bounds")
    butterfly(after)
    return values


def masks_of(lane, crosses, bits):
    return [((lane >> bit) & 1) * cross == 1 for cross, bit in zip(crosses, bits, strict=True)]


def lanes_of(lane, crosses, bits):
    moves = [cross << bit for cross, bit in zip(crosses, bits, strict=True)]
    offsets = [jnp.int32(0)]
    for move in moves:
        offsets += [offset | move for offset in offsets]
    return [jnp.bitwise_xor(lane, offset) for offset in offsets]


def first_kernel(lo_bits, order_hbm, gate_hbm, x_hbm, gates_hbm, *refs):
    outs, (order_ref, gate_ref, x_ref, gates_ref, work, sems) = refs[:-6], refs[-6:]
    outs, (coefs_out, lanes_out) = outs[:-2], outs[-2:]
    parts = 1 << lo_bits
    fetches = [
        pltpu.make_async_copy(order_hbm, order_ref, sems.at[0]),
        pltpu.make_async_copy(gates_hbm.at[pl.ds(0, 2)], gates_ref, sems.at[1]),
        pltpu.make_async_copy(x_hbm, x_ref, sems.at[2]),
        pltpu.make_async_copy(gate_hbm, gate_ref, sems.at[3]),
    ]
    for fetch in fetches:
        fetch.start()
    fetches[0].wait()
    order = [order_ref[k] for k in range(LANE_BITS + ROW_BITS)]
    crosses, wanted, slots, row_before, lane_before, new_in_lane = plan_of(order, lo_bits)
    index = lax.broadcasted_iota(jnp.int32, (1, 2 * WIDTH), 1)
    rows = one_hot(2 * WIDTH, moved_bits(index, row_before, range(ROW_BITS)))
    lane = lax.broadcasted_iota(jnp.int32, (8, WIDTH), 1)
    lanes_out[...] = moved_bits(lane, range(LANE_BITS), new_in_lane)
    old_lane = moved_bits(lane, range(LANE_BITS), lane_before)
    fetches[1].wait()
    real, imag = halves(gates_ref[0, 0]), halves(gates_ref[0, 1])
    matrix0 = [block_matrix(real[i], imag[i]) for i in range(2)]
    real, imag = halves(gates_ref[1, 0]), halves(gates_ref[1, 1])
    matrix1 = [block_matrix(real[i], imag[i]) for i in range(2)]
    fetches[2].wait()
    pieces = [[x_ref[pl.ds(m * 2 + c, WIDTH, stride=4), :] for m in range(2)] for c in range(2)]
    state = jnp.concatenate([jnp.concatenate(row, axis=1) for row in pieces], axis=0)
    state = dot3(matrix0, halves(state))
    state = [dot(rows, half).astype(BF16) for half in halves(turned(state))]
    state = dot3(state, matrix1, transposed=True)
    before, after = masks_of(lane, crosses[3:], wanted[3:]), masks_of(lane, crosses[3:], slots[3:])
    index = lanes_of(old_lane, crosses[3:], wanted[3:])
    for c in range(2):
        values = [state[8 * v : 8 * v + 8, c * WIDTH : (c + 1) * WIDTH] for v in range(32)]
        for v, value in enumerate(crossed(values, before, after, index)):
            work[c, pl.ds(8 * v, 8), :] = value
    masks = masks_of(lane, crosses[:3], slots[:3])
    index = lanes_of(lane, crosses[:3], slots[:3])
    for c in range(2):
        for group in range(4):
            places = [pl.ds(group * 64 + o, 8, stride=8) for o in range(8)]
            values = crossed([work[c, place, :] for place in places], masks, masks, index)
            for place, value in zip(places, values, strict=True):
                work[c, place, :] = value
    me = lax.axis_index("lo")
    count = 2 * WIDTH // parts
    near = outs[0].shape[0]
    for step in range(parts):
        out = outs[0].at[step] if step < near else outs[1 + step - near]
        source = pl.multiple_of(jnp.bitwise_xor(me, step) * count, 8)
        for c in range(2):
            out[c] = work[c, pl.ds(source, count), :]
    fetches[3].wait()
    side = jnp.right_shift(lax.axis_index("hi"), lax.axis_size("hi").bit_length() - 2) & 1
    for other in range(2):
        for c in range(2):
            coefs_out[2 * other + c] = jnp.full((8, WIDTH), gate_ref[c, side, side ^ other])


def turned(value):
    return jnp.concatenate(
        [
            jnp.concatenate([value[i * WIDTH : (i + 1) * WIDTH, j * WIDTH : (j + 1) * WIDTH] for i in range(2)], axis=1)
            for j in range(2)
        ],
        axis=0,
    )


def mixed(coefs_ref, own, other):
    own_r, own_i, other_r, other_i = [jnp.concatenate([coefs_ref[i]] * (own.shape[-2] // 8), axis=0) for i in range(4)]
    return (
        own_r * own[0] - own_i * own[1] + (other_r * other[0] - other_i * other[1]),
        own_r * own[1] + own_i * own[0] + (other_r * other[1] + other_i * other[0]),
    )


def mix_kernel(coefs_ref, matrix_ref, own_ref, other_ref, *outs):
    values = [mixed(coefs_ref, own_ref.at[k + 1], other_ref.at[k + 1]) for k in range(len(outs))]
    for out_ref, value in zip(outs, low_gate(matrix_ref, values), strict=True):
        out_ref[0], out_ref[1] = value


def arrival(parts):
    near = parts // 2
    return [0, *range(near, parts - 1)], [*range(1, near), parts - 1]


def low_weights_kernel(lanes_ref, gates_hbm, out_ref, gate_ref, sem):
    fetch = pltpu.make_async_copy(gates_hbm.at[3], gate_ref, sem)
    fetch.start()
    lanes = one_hot(WIDTH, lanes_ref[0:1])
    fetch.wait()
    for i in range(2):
        real, imag = [dot(halves(gate_ref[c])[i], lanes).T for c in range(2)]
        out_ref[i] = block_matrix(real, -imag).astype(BF16)


def high_weights_kernel(lo_bits, gates_hbm, early_ref, late_ref, gates_ref, sems):
    fetches = [pltpu.make_async_copy(gates_hbm.at[2 + 2 * g], gates_ref.at[g], sems.at[g]) for g in range(2)]
    for fetch in fetches:
        fetch.start()
    parts = 1 << lo_bits
    kept = WIDTH // parts
    me = lax.axis_index("lo")
    index = lax.broadcasted_iota(jnp.int32, (1, WIDTH), 1)
    source = index % kept
    early, late = arrival(parts)
    for place, step in enumerate(early + late):
        source = source + jnp.where(index // kept == place, jnp.bitwise_xor(me, step) * kept, 0)
    rows = one_hot(WIDTH, source)
    for fetch in fetches:
        fetch.wait()

    def exact(left, right):
        return lax.dot_general(
            left, right, (((1,), (0,)), ((), ())), precision=lax.Precision.HIGHEST, preferred_element_type=F32
        )

    first, last = [[gates_ref[g, c] for c in range(2)] for g in range(2)]
    real = halves(exact(last[0], first[0]) - exact(last[1], first[1]))
    imag = halves(exact(last[0], first[1]) + exact(last[1], first[0]))
    half = len(early) * kept
    for i in range(2):
        both = [dot(part[i], rows) for part in (real, imag)]
        early_ref[i] = block_matrix(*[part[:, :half] for part in both]).astype(BF16)
        late_ref[i] = block_matrix(*[part[:, half:] for part in both]).astype(BF16)


def low_gate(matrix_ref, values):
    state = jnp.concatenate([jnp.concatenate(value, axis=1) for value in values], axis=0)
    state = dot3(halves(state), (matrix_ref[0], matrix_ref[1]))
    count = state.shape[0] // len(values)
    return [
        [state[i * count : (i + 1) * count, c * WIDTH : (c + 1) * WIDTH] for c in range(2)] for i in range(len(values))
    ]


def for_high(values):
    kept = values[0][0].shape[0] // 2
    return jnp.concatenate(
        [
            jnp.concatenate([value[c][m * kept : (m + 1) * kept] for m in range(2)], axis=1)
            for c in range(2)
            for value in values
        ],
        axis=0,
    )


def copy_kernel(in_ref, out_ref):
    out_ref[...] = in_ref[...]


def low_kernel(matrix_ref, in_ref, out_ref):
    (value,) = low_gate(matrix_ref, [(in_ref[0], in_ref[1])])
    out_ref[0], out_ref[1] = value


def early_kernel(coefs_ref, low_gate_ref, high_gate_ref, near_own_ref, near_other_ref, *refs):
    ins, out_ref = refs[:-1], refs[-1]
    values = [mixed(coefs_ref, near_own_ref.at[0], near_other_ref.at[0])]
    values += [mixed(coefs_ref, own, other) for own, other in zip(ins[0::2], ins[1::2], strict=True)]
    out_ref[...] = dot3((high_gate_ref[0], high_gate_ref[1]), halves(for_high(low_gate(low_gate_ref, values))))


def last_kernel(coefs_ref, high_gate_ref, early_ref, own_ref, other_ref, *refs):
    ins, (out_hbm, out_ref, sems) = refs[:-3], refs[-3:]
    values = [(ref[0], ref[1]) for ref in ins] + [mixed(coefs_ref, own_ref, other_ref)]
    high, low = halves(for_high(values))
    state = jnp.concatenate([low, high, high], axis=0)
    sends = []
    half = WIDTH // 2
    for i in range(2):
        matrix = [
            jnp.concatenate(
                [high_gate_ref[j, c * WIDTH + i * half : c * WIDTH + (i + 1) * half] for c in range(2)], axis=0
            )
            for j in (0, 1, 0)
        ]
        result = dot(jnp.concatenate(matrix, axis=1), state)
        for c in range(2):
            for m in range(2):
                at = c * WIDTH + i * half
                out_ref[pl.ds(i * 256 + m * 2 + c, half, stride=4), :] = (
                    early_ref[at : at + half, m * WIDTH : (m + 1) * WIDTH]
                    + result[c * half : (c + 1) * half, m * WIDTH : (m + 1) * WIDTH]
                )
        sends.append(
            pltpu.make_async_copy(out_ref.at[pl.ds(i * 256, 256)], out_hbm.at[pl.ds(i * 256, 256)], sems.at[i])
        )
        sends[-1].start()
    for send in sends:
        send.wait()


def swapped(block, axis, distance):
    count = lax.axis_size(axis)
    return lax.ppermute(block, axis, [(i, i ^ distance) for i in range(count)])


PARAMS = pltpu.CompilerParams(vmem_limit_bytes=8 << 20)
HBM = pl.BlockSpec(memory_space=pltpu.HBM)
VMEM = pl.BlockSpec(memory_space=pltpu.VMEM)


def in_hbm(value):
    return pltpu.with_memory_space_constraint(value, pltpu.HBM)


def on_device(amplitudes, gate_mats, dev_gate, qubit_order):
    parts = lax.axis_size("lo")
    lo_bits = parts.bit_length() - 1
    top = lax.axis_size("hi") // 2
    kept = WIDTH // parts
    rows = amplitudes.reshape(2, 256, WIDTH).transpose(1, 0, 2).reshape(512, WIDTH)
    block = pltpu.VMEM((2, 2 * kept, WIDTH), F32)
    near = parts // 2
    near_own, *far_own, coefs, lanes = pl.pallas_call(
        functools.partial(first_kernel, lo_bits),
        out_shape=[pltpu.VMEM((near, 2, 2 * kept, WIDTH), F32)]
        + [block] * (parts - near)
        + [pltpu.VMEM((4, 8, WIDTH), F32), pltpu.VMEM((8, WIDTH), jnp.int32)],
        in_specs=[HBM] * 4,
        out_specs=[VMEM] * (parts - near + 3),
        scratch_shapes=[
            pltpu.SMEM((LANE_BITS + ROW_BITS,), jnp.int32),
            pltpu.SMEM((2, 2, 2), F32),
            pltpu.VMEM((512, WIDTH), F32),
            pltpu.VMEM((2, 2, WIDTH, WIDTH), F32),
            pltpu.VMEM((2, 256, WIDTH), F32),
            pltpu.SemaphoreType.DMA((4,)),
        ],
        compiler_params=PARAMS,
        name="first_gates",
    )(in_hbm(qubit_order), in_hbm(dev_gate), in_hbm(rows), in_hbm(gate_mats))
    near_other = swapped(near_own, "hi", top)
    far_own = [swapped(far, "lo", near + i) for i, far in enumerate(far_own)]
    counts = [2 * kept * len(steps) for steps in arrival(parts)]
    low_weights = pl.pallas_call(
        low_weights_kernel,
        out_shape=pltpu.VMEM((2, 256, 256), BF16),
        in_specs=[VMEM, HBM],
        out_specs=VMEM,
        scratch_shapes=[pltpu.VMEM((2, WIDTH, WIDTH), F32), pltpu.SemaphoreType.DMA],
        compiler_params=PARAMS,
        name="low_weights",
    )(lanes, in_hbm(gate_mats))
    early_weights, late_weights = pl.pallas_call(
        functools.partial(high_weights_kernel, lo_bits),
        out_shape=[pltpu.VMEM((2, 256, count), BF16) for count in counts],
        in_specs=[HBM],
        out_specs=[VMEM] * 2,
        scratch_shapes=[pltpu.VMEM((2, 2, WIDTH, WIDTH), F32), pltpu.SemaphoreType.DMA((2,))],
        compiler_params=PARAMS,
        name="high_weights",
    )(in_hbm(gate_mats))
    far_own[-1] = pl.pallas_call(
        low_kernel, out_shape=block, in_specs=[VMEM] * 2, out_specs=VMEM, compiler_params=PARAMS, name="low_gate"
    )(low_weights, far_own[-1])
    far_other = [swapped(far, "hi", top) for far in far_own]
    far_other[0] = pl.pallas_call(
        copy_kernel, out_shape=block, in_specs=[VMEM], out_specs=VMEM, compiler_params=PARAMS, name="arrived"
    )(far_other[0])
    mixes = pl.pallas_call(
        mix_kernel,
        out_shape=[block] * (near - 1),
        in_specs=[VMEM] * 4,
        out_specs=[VMEM] * (near - 1),
        compiler_params=PARAMS,
        name="mix_pair",
    )(coefs, low_weights, near_own, near_other)
    mixes = [swapped(mix, "lo", 1 + i) for i, mix in enumerate(mixes)]
    pairs = [value for pair in zip(far_own[:-1], far_other[:-1], strict=True) for value in pair]
    early = pl.pallas_call(
        early_kernel,
        out_shape=pltpu.VMEM((256, 256), F32),
        in_specs=[VMEM] * (5 + len(pairs)),
        out_specs=VMEM,
        compiler_params=PARAMS,
        name="early_gate",
    )(coefs, low_weights, early_weights, near_own, near_other, *pairs)
    out = pl.pallas_call(
        last_kernel,
        out_shape=jax.ShapeDtypeStruct((512, WIDTH), F32),
        in_specs=[VMEM] * (5 + len(mixes)),
        out_specs=HBM,
        scratch_shapes=[pltpu.VMEM((512, WIDTH), F32), pltpu.SemaphoreType.DMA((2,))],
        compiler_params=PARAMS,
        name="last_gates",
    )(coefs, late_weights, early, far_own[-1], far_other[-1], *mixes)
    return out.reshape(256, 2, WIDTH).transpose(1, 0, 2).reshape(2, -1)


def solution(mesh):
    return jax.shard_map(
        on_device,
        mesh=mesh,
        in_specs=(P(None, ("hi", "lo")), P(), P(), P()),
        out_specs=P(None, ("hi", "lo")),
        check_vma=False,
    )
```

```python
import functools

import jax
import jax.numpy as jnp
from jax import lax
from jax.experimental import pallas as pl
from jax.experimental.pallas import tpu as pltpu
from jax.sharding import PartitionSpec as P

WIDTH = 128
LANE_BITS = 7
ROW_BITS = 8
F32, BF16 = jnp.float32, jnp.bfloat16


def halves(value):
    high = value.astype(BF16)
    return high, (value - high.astype(F32)).astype(BF16)


def dot(left, right, transposed=False):
    return lax.dot_general(
        left, right, (((1,), (1 if transposed else 0,)), ((), ())), preferred_element_type=F32
    )


def dot3(left, right, transposed=False):
    (lh, ll), (rh, rl) = left, right
    return dot(lh, rl, transposed) + dot(ll, rh, transposed) + dot(lh, rh, transposed)


def block_matrix(real, imag):
    return jnp.concatenate(
        [jnp.concatenate([real, -imag], axis=1), jnp.concatenate([imag, real], axis=1)], axis=0
    )


def new_positions(lo_bits):
    kept = LANE_BITS - lo_bits
    return [8 + r for r in range(kept)] + [7] + [8 + r for r in range(kept, LANE_BITS)]


def plan_of(order, lo_bits):
    one, zero = jnp.int32(1), jnp.int32(0)
    middle = LANE_BITS - lo_bits
    row_of_lane = [l if l < middle else l + 1 for l in range(LANE_BITS)]
    wanted = [order[k] for k in new_positions(lo_bits)]
    crosses = [jnp.where(w < LANE_BITS, one, zero) for w in wanted]
    crosses_middle = crosses[middle]
    used, before = [], zero
    spare = zero
    for l in range(LANE_BITS):
        free = (one - crosses[row_of_lane[l]]) * crosses_middle * jnp.where(before == 0, one, zero)
        spare = spare + free * l
        used.append(crosses[row_of_lane[l]] + free)
        before = before + free
    key_lane, moved, stayed = [], zero, zero
    for l in range(LANE_BITS):
        key_lane.append(jnp.where(used[l] == 1, moved + 16, stayed))
        moved, stayed = moved + used[l], stayed + (one - used[l])
    key_new, moved, stayed = [], zero, zero
    for k in range(LANE_BITS):
        from_row = jnp.where(order[k] >= LANE_BITS, one, zero)
        key_new.append(jnp.where(from_row == 1, moved + 16, stayed))
        moved, stayed = moved + from_row, stayed + (one - from_row)
    match = []
    for l in range(LANE_BITS):
        total = zero
        for k in range(LANE_BITS):
            total = total + jnp.where(key_lane[l] == key_new[k], order[k] + 16 * k, zero)
        match.append(total)
    new_in_lane = [m >> 4 for m in match]
    lane_before, row_before = [], [None] * ROW_BITS
    middle_before = zero
    for l in range(LANE_BITS):
        r = row_of_lane[l]
        old = match[l] & 15
        at_spare = crosses_middle * jnp.where(spare == l, one, zero)
        lane_before.append(jnp.where(crosses[r] == 1, wanted[r], jnp.where(at_spare == 1, wanted[middle], old)))
        row_before[r] = jnp.where(crosses[r] == 1, old, wanted[r]) & 7
        middle_before = middle_before + at_spare * old
    row_before[middle] = jnp.where(crosses_middle == 1, middle_before, wanted[middle]) & 7
    slots = [r if r < middle else r - 1 for r in range(ROW_BITS)]
    slots[middle] = spare
    return crosses, wanted, slots, row_before, lane_before, new_in_lane


def middle_high(plan):
    crosses, wanted, slots, row_before = plan
    place = jnp.int32(3)
    for r in range(3):
        place = jnp.where(row_before[r] == LANE_BITS, r, place)

    def exchanged(values):
        values = [jnp.int32(value) for value in values]
        moved = values[3]
        for r in range(3):
            moved = jnp.where(place == r, values[r], moved)
        return [jnp.where(place == r, values[3], values[r]) for r in range(3)] + [moved] + values[4:]

    return *(exchanged(values) for values in (crosses, wanted, slots, row_before)), place


def moved_bits(index, sources, targets):
    total = jnp.zeros_like(index)
    for source, target in zip(sources, targets, strict=True):
        total = total | (((index >> source) & 1) << target)
    return total


def one_hot(count, index):
    rows = lax.broadcasted_iota(jnp.int32, (count, index.shape[1]), 0)
    return jnp.where(rows == index, 1.0, 0.0).astype(F32).astype(BF16)


def crossed(values, before, after, index):
    values = list(values)

    def butterfly(masks):
        for bit, mask in enumerate(masks):
            for i in range(len(values)):
                if not i >> bit & 1:
                    low, high = values[i], values[i | 1 << bit]
                    values[i] = jnp.where(mask, high, low)
                    values[i | 1 << bit] = jnp.where(mask, low, high)

    butterfly(before)
    for i, lanes in enumerate(index):
        values[i] = jnp.take_along_axis(values[i], lanes, axis=1, mode="promise_in_bounds")
    butterfly(after)
    return values


def masks_of(lane, crosses, bits):
    return [((lane >> bit) & 1) * cross == 1 for cross, bit in zip(crosses, bits, strict=True)]


def lanes_of(lane, crosses, bits):
    moves = [cross << bit for cross, bit in zip(crosses, bits, strict=True)]
    offsets = [jnp.int32(0)]
    for move in moves:
        offsets += [offset | move for offset in offsets]
    return [jnp.bitwise_xor(lane, offset) for offset in offsets]


def first_kernel(lo_bits, order_hbm, gate_hbm, x_hbm, gates_hbm, *refs):
    outs, (order_ref, gate_ref, x_ref, gates_ref, work, sems) = refs[:-6], refs[-6:]
    outs, (coefs_out, orders_out) = outs[:-2], outs[-2:]
    parts = 1 << lo_bits
    fetches = [
        pltpu.make_async_copy(order_hbm, order_ref, sems.at[0]),
        pltpu.make_async_copy(gates_hbm.at[pl.ds(0, 2)], gates_ref, sems.at[1]),
        pltpu.make_async_copy(x_hbm, x_ref, sems.at[2]),
        pltpu.make_async_copy(gate_hbm, gate_ref, sems.at[3]),
    ]
    for fetch in fetches:
        fetch.start()
    fetches[0].wait()
    order = [order_ref[k] for k in range(LANE_BITS + ROW_BITS)]
    *plan, lane_before, new_in_lane = plan_of(order, lo_bits)
    folded = lo_bits + 3 < LANE_BITS
    place = jnp.int32(3)
    if folded:
        *plan, place = middle_high(plan)
    crosses, wanted, slots, row_before = plan
    lane = lax.broadcasted_iota(jnp.int32, (8, WIDTH), 1)
    orders_out[0] = moved_bits(lane, range(LANE_BITS), new_in_lane)
    turn = [jnp.where(place == r, 3, r) for r in range(3)] + [place] + [*range(4, LANE_BITS)]
    orders_out[1] = moved_bits(lane, range(LANE_BITS), turn)
    if folded:
        middle = jnp.int32(0)
        for r in range(ROW_BITS):
            middle = jnp.where(row_before[r] == LANE_BITS, r, middle)
        after_middle = [jnp.where(middle < r, 1, 0) for r in range(ROW_BITS)]
        index = lax.broadcasted_iota(jnp.int32, (1, WIDTH), 1)
        rows = one_hot(WIDTH, moved_bits(index, row_before, [r - after_middle[r] for r in range(ROW_BITS)]))
        offsets = [jnp.int32(0)]
        for r in range(3, ROW_BITS):
            stride = jnp.where(middle == r, WIDTH, jnp.left_shift(1, r - after_middle[r]))
            offsets += [offset + stride for offset in offsets]
    else:
        index = lax.broadcasted_iota(jnp.int32, (1, 2 * WIDTH), 1)
        rows = one_hot(2 * WIDTH, moved_bits(index, row_before, range(ROW_BITS)))
    old_lane = moved_bits(lane, range(LANE_BITS), lane_before)
    fetches[1].wait()
    fetches[2].wait()
    fetches[3].wait()
    real, imag = halves(gates_ref[0, 0]), halves(gates_ref[0, 1])
    if folded:
        both = [dot(rows, jnp.concatenate([real[i], imag[i]], axis=1)).astype(BF16) for i in range(2)]
        real, imag = [[half[:, c * WIDTH : (c + 1) * WIDTH] for half in both] for c in range(2)]
    matrix0 = [block_matrix(real[i], imag[i]) for i in range(2)]
    real, imag = halves(gates_ref[1, 0]), halves(gates_ref[1, 1])
    matrix1 = [block_matrix(real[i], imag[i]) for i in range(2)]
    pieces = [[x_ref[pl.ds(m * 2 + c, WIDTH, stride=4), :] for m in range(2)] for c in range(2)]
    state = jnp.concatenate([jnp.concatenate(row, axis=1) for row in pieces], axis=0)
    state = dot3(matrix0, halves(state))
    if folded:
        for c in range(2):
            for m in range(2):
                work[c, m * WIDTH : (m + 1) * WIDTH] = state[c * WIDTH : (c + 1) * WIDTH, m * WIDTH : (m + 1) * WIDTH]
        state = halves(
            jnp.concatenate(
                [
                    jnp.concatenate([work[c, pl.ds(pl.multiple_of(offset, 8), 8), :] for offset in offsets], axis=0)
                    for c in range(2)
                ],
                axis=1,
            )
        )
    else:
        state = [dot(rows, half).astype(BF16) for half in halves(turned(state))]
    state = dot3(state, matrix1, transposed=True)
    before, after = masks_of(lane, crosses[3:], wanted[3:]), masks_of(lane, crosses[3:], slots[3:])
    index = lanes_of(old_lane, crosses[3:], wanted[3:])
    for c in range(2):
        values = [state[8 * v : 8 * v + 8, c * WIDTH : (c + 1) * WIDTH] for v in range(32)]
        for v, value in enumerate(crossed(values, before, after, index)):
            work[c, pl.ds(8 * v, 8), :] = value
    masks = masks_of(lane, crosses[:3], slots[:3])
    index = lanes_of(lane, crosses[:3], slots[:3])
    for c in range(2):
        for group in range(4):
            places = [pl.ds(group * 64 + o, 8, stride=8) for o in range(8)]
            values = crossed([work[c, place, :] for place in places], masks, masks, index)
            for place, value in zip(places, values, strict=True):
                work[c, place, :] = value
    me = lax.axis_index("lo")
    count = 2 * WIDTH // parts
    near = outs[0].shape[0]
    for step in range(parts):
        out = outs[0].at[step] if step < near else outs[1 + step - near]
        source = pl.multiple_of(jnp.bitwise_xor(me, step) * count, 8)
        for c in range(2):
            out[c] = work[c, pl.ds(source, count), :]
    side = jnp.right_shift(lax.axis_index("hi"), lax.axis_size("hi").bit_length() - 2) & 1
    for other in range(2):
        for c in range(2):
            coefs_out[2 * other + c] = jnp.full((8, WIDTH), gate_ref[c, side, side ^ other])


def turned(value):
    return jnp.concatenate(
        [
            jnp.concatenate([value[i * WIDTH : (i + 1) * WIDTH, j * WIDTH : (j + 1) * WIDTH] for i in range(2)], axis=1)
            for j in range(2)
        ],
        axis=0,
    )


def mixed(coefs_ref, own, other):
    own_r, own_i, other_r, other_i = [jnp.concatenate([coefs_ref[i]] * (own.shape[-2] // 8), axis=0) for i in range(4)]
    return (
        own_r * own[0] - own_i * own[1] + (other_r * other[0] - other_i * other[1]),
        own_r * own[1] + own_i * own[0] + (other_r * other[1] + other_i * other[0]),
    )


def mix_kernel(coefs_ref, matrix_ref, own_ref, other_ref, *outs):
    values = [mixed(coefs_ref, own_ref.at[k + 1], other_ref.at[k + 1]) for k in range(len(outs))]
    for out_ref, value in zip(outs, low_gate(matrix_ref, values), strict=True):
        out_ref[0], out_ref[1] = value


def arrival(parts):
    near = parts // 2
    return [0, *range(near, parts - 1)], [*range(1, near), parts - 1]


def low_weights_kernel(orders_ref, gates_hbm, out_ref, gate_ref, sem):
    fetch = pltpu.make_async_copy(gates_hbm.at[3], gate_ref, sem)
    fetch.start()
    lanes = one_hot(WIDTH, orders_ref[0, 0:1])
    fetch.wait()
    for i in range(2):
        real, imag = [dot(halves(gate_ref[c])[i], lanes).T for c in range(2)]
        out_ref[i] = block_matrix(real, -imag).astype(BF16)


def high_weights_kernel(lo_bits, orders_ref, gates_hbm, early_ref, late_ref, gates_ref, sems):
    fetches = [pltpu.make_async_copy(gates_hbm.at[2 + 2 * g], gates_ref.at[g], sems.at[g]) for g in range(2)]
    for fetch in fetches:
        fetch.start()
    parts = 1 << lo_bits
    kept = WIDTH // parts
    me = lax.axis_index("lo")
    index = lax.broadcasted_iota(jnp.int32, (1, WIDTH), 1)
    source = orders_ref[1, 0:1] % kept
    early, late = arrival(parts)
    for place, step in enumerate(early + late):
        source = source + jnp.where(index // kept == place, jnp.bitwise_xor(me, step) * kept, 0)
    rows = one_hot(WIDTH, source)
    for fetch in fetches:
        fetch.wait()

    def exact(left, right):
        return lax.dot_general(
            left, right, (((1,), (0,)), ((), ())), precision=lax.Precision.HIGHEST, preferred_element_type=F32
        )

    first, last = [[gates_ref[g, c] for c in range(2)] for g in range(2)]
    real = halves(exact(last[0], first[0]) - exact(last[1], first[1]))
    imag = halves(exact(last[0], first[1]) + exact(last[1], first[0]))
    half = len(early) * kept
    for i in range(2):
        both = [dot(part[i], rows) for part in (real, imag)]
        early_ref[i] = block_matrix(*[part[:, :half] for part in both]).astype(BF16)
        late_ref[i] = block_matrix(*[part[:, half:] for part in both]).astype(BF16)


def low_gate(matrix_ref, values):
    state = jnp.concatenate([jnp.concatenate(value, axis=1) for value in values], axis=0)
    state = dot3(halves(state), (matrix_ref[0], matrix_ref[1]))
    count = state.shape[0] // len(values)
    return [
        [state[i * count : (i + 1) * count, c * WIDTH : (c + 1) * WIDTH] for c in range(2)] for i in range(len(values))
    ]


def for_high(values):
    kept = values[0][0].shape[0] // 2
    return jnp.concatenate(
        [
            jnp.concatenate([value[c][m * kept : (m + 1) * kept] for m in range(2)], axis=1)
            for c in range(2)
            for value in values
        ],
        axis=0,
    )


def copy_kernel(in_ref, out_ref):
    out_ref[...] = in_ref[...]


def low_kernel(matrix_ref, in_ref, out_ref):
    (value,) = low_gate(matrix_ref, [(in_ref[0], in_ref[1])])
    out_ref[0], out_ref[1] = value


def early_kernel(coefs_ref, low_gate_ref, high_gate_ref, near_own_ref, near_other_ref, *refs):
    ins, out_ref = refs[:-1], refs[-1]
    values = [mixed(coefs_ref, near_own_ref.at[0], near_other_ref.at[0])]
    values += [mixed(coefs_ref, own, other) for own, other in zip(ins[0::2], ins[1::2], strict=True)]
    out_ref[...] = dot3((high_gate_ref[0], high_gate_ref[1]), halves(for_high(low_gate(low_gate_ref, values))))


def last_kernel(coefs_ref, high_gate_ref, early_ref, own_ref, other_ref, *refs):
    ins, (out_hbm, out_ref, sems) = refs[:-3], refs[-3:]
    values = [(ref[0], ref[1]) for ref in ins] + [mixed(coefs_ref, own_ref, other_ref)]
    high, low = halves(for_high(values))
    state = jnp.concatenate([low, high, high], axis=0)
    sends = []
    half = WIDTH // 2
    for i in range(2):
        matrix = [
            jnp.concatenate(
                [high_gate_ref[j, c * WIDTH + i * half : c * WIDTH + (i + 1) * half] for c in range(2)], axis=0
            )
            for j in (0, 1, 0)
        ]
        result = dot(jnp.concatenate(matrix, axis=1), state)
        for c in range(2):
            for m in range(2):
                at = c * WIDTH + i * half
                out_ref[pl.ds(i * 256 + m * 2 + c, half, stride=4), :] = (
                    early_ref[at : at + half, m * WIDTH : (m + 1) * WIDTH]
                    + result[c * half : (c + 1) * half, m * WIDTH : (m + 1) * WIDTH]
                )
        sends.append(
            pltpu.make_async_copy(out_ref.at[pl.ds(i * 256, 256)], out_hbm.at[pl.ds(i * 256, 256)], sems.at[i])
        )
        sends[-1].start()
    for send in sends:
        send.wait()


def swapped(block, axis, distance):
    count = lax.axis_size(axis)
    return lax.ppermute(block, axis, [(i, i ^ distance) for i in range(count)])


PARAMS = pltpu.CompilerParams(vmem_limit_bytes=8 << 20)
HBM = pl.BlockSpec(memory_space=pltpu.HBM)
VMEM = pl.BlockSpec(memory_space=pltpu.VMEM)


def in_hbm(value):
    return pltpu.with_memory_space_constraint(value, pltpu.HBM)


def on_device(amplitudes, gate_mats, dev_gate, qubit_order):
    parts = lax.axis_size("lo")
    lo_bits = parts.bit_length() - 1
    top = lax.axis_size("hi") // 2
    kept = WIDTH // parts
    rows = amplitudes.reshape(2, 256, WIDTH).transpose(1, 0, 2).reshape(512, WIDTH)
    block = pltpu.VMEM((2, 2 * kept, WIDTH), F32)
    near = parts // 2
    near_own, *far_own, coefs, orders = pl.pallas_call(
        functools.partial(first_kernel, lo_bits),
        out_shape=[pltpu.VMEM((near, 2, 2 * kept, WIDTH), F32)]
        + [block] * (parts - near)
        + [pltpu.VMEM((4, 8, WIDTH), F32), pltpu.VMEM((2, 8, WIDTH), jnp.int32)],
        in_specs=[HBM] * 4,
        out_specs=[VMEM] * (parts - near + 3),
        scratch_shapes=[
            pltpu.SMEM((LANE_BITS + ROW_BITS,), jnp.int32),
            pltpu.SMEM((2, 2, 2), F32),
            pltpu.VMEM((512, WIDTH), F32),
            pltpu.VMEM((2, 2, WIDTH, WIDTH), F32),
            pltpu.VMEM((2, 256, WIDTH), F32),
            pltpu.SemaphoreType.DMA((4,)),
        ],
        compiler_params=PARAMS,
        name="first_gates",
    )(in_hbm(qubit_order), in_hbm(dev_gate), in_hbm(rows), in_hbm(gate_mats))
    near_other = swapped(near_own, "hi", top)
    far_own = [swapped(far, "lo", near + i) for i, far in enumerate(far_own)]
    counts = [2 * kept * len(steps) for steps in arrival(parts)]
    low_weights = pl.pallas_call(
        low_weights_kernel,
        out_shape=pltpu.VMEM((2, 256, 256), BF16),
        in_specs=[VMEM, HBM],
        out_specs=VMEM,
        scratch_shapes=[pltpu.VMEM((2, WIDTH, WIDTH), F32), pltpu.SemaphoreType.DMA],
        compiler_params=PARAMS,
        name="low_weights",
    )(orders, in_hbm(gate_mats))
    early_weights, late_weights = pl.pallas_call(
        functools.partial(high_weights_kernel, lo_bits),
        out_shape=[pltpu.VMEM((2, 256, count), BF16) for count in counts],
        in_specs=[VMEM, HBM],
        out_specs=[VMEM] * 2,
        scratch_shapes=[pltpu.VMEM((2, 2, WIDTH, WIDTH), F32), pltpu.SemaphoreType.DMA((2,))],
        compiler_params=PARAMS,
        name="high_weights",
    )(orders, in_hbm(gate_mats))
    far_own[-1] = pl.pallas_call(
        low_kernel, out_shape=block, in_specs=[VMEM] * 2, out_specs=VMEM, compiler_params=PARAMS, name="low_gate"
    )(low_weights, far_own[-1])
    far_other = [swapped(far, "hi", top) for far in far_own]
    far_other[0] = pl.pallas_call(
        copy_kernel, out_shape=block, in_specs=[VMEM], out_specs=VMEM, compiler_params=PARAMS, name="arrived"
    )(far_other[0])
    mixes = pl.pallas_call(
        mix_kernel,
        out_shape=[block] * (near - 1),
        in_specs=[VMEM] * 4,
        out_specs=[VMEM] * (near - 1),
        compiler_params=PARAMS,
        name="mix_pair",
    )(coefs, low_weights, near_own, near_other)
    mixes = [swapped(mix, "lo", 1 + i) for i, mix in enumerate(mixes)]
    pairs = [value for pair in zip(far_own[:-1], far_other[:-1], strict=True) for value in pair]
    early = pl.pallas_call(
        early_kernel,
        out_shape=pltpu.VMEM((256, 256), F32),
        in_specs=[VMEM] * (5 + len(pairs)),
        out_specs=VMEM,
        compiler_params=PARAMS,
        name="early_gate",
    )(coefs, low_weights, early_weights, near_own, near_other, *pairs)
    out = pl.pallas_call(
        last_kernel,
        out_shape=jax.ShapeDtypeStruct((512, WIDTH), F32),
        in_specs=[VMEM] * (5 + len(mixes)),
        out_specs=HBM,
        scratch_shapes=[pltpu.VMEM((512, WIDTH), F32), pltpu.SemaphoreType.DMA((2,))],
        compiler_params=PARAMS,
        name="last_gates",
    )(coefs, late_weights, early, far_own[-1], far_other[-1], *mixes)
    return out.reshape(256, 2, WIDTH).transpose(1, 0, 2).reshape(2, -1)


def solution(mesh):
    return jax.shard_map(
        on_device,
        mesh=mesh,
        in_specs=(P(None, ("hi", "lo")), P(), P(), P()),
        out_specs=P(None, ("hi", "lo")),
        check_vma=False,
    )
```

```python
import functools

import jax
import jax.numpy as jnp
from jax import lax
from jax.experimental import pallas as pl
from jax.experimental.pallas import tpu as pltpu
from jax.sharding import PartitionSpec as P

WIDTH = 128
LANE_BITS = 7
ROW_BITS = 8
F32, BF16 = jnp.float32, jnp.bfloat16


def halves(value):
    high = value.astype(BF16)
    return high, (value - high.astype(F32)).astype(BF16)


def dot(left, right, transposed=False):
    return lax.dot_general(
        left, right, (((1,), (1 if transposed else 0,)), ((), ())), preferred_element_type=F32
    )


def dot3(left, right, transposed=False):
    (lh, ll), (rh, rl) = left, right
    return dot(lh, rl, transposed) + dot(ll, rh, transposed) + dot(lh, rh, transposed)


def block_matrix(real, imag):
    return jnp.concatenate(
        [jnp.concatenate([real, -imag], axis=1), jnp.concatenate([imag, real], axis=1)], axis=0
    )


def new_positions(lo_bits):
    kept = LANE_BITS - lo_bits
    return [8 + r for r in range(kept)] + [7] + [8 + r for r in range(kept, LANE_BITS)]


def plan_of(order, lo_bits):
    one, zero = jnp.int32(1), jnp.int32(0)
    middle = LANE_BITS - lo_bits
    row_of_lane = [l if l < middle else l + 1 for l in range(LANE_BITS)]
    wanted = [order[k] for k in new_positions(lo_bits)]
    crosses = [jnp.where(w < LANE_BITS, one, zero) for w in wanted]
    crosses_middle = crosses[middle]
    used, before = [], zero
    spare = zero
    for l in range(LANE_BITS):
        free = (one - crosses[row_of_lane[l]]) * crosses_middle * jnp.where(before == 0, one, zero)
        spare = spare + free * l
        used.append(crosses[row_of_lane[l]] + free)
        before = before + free
    key_lane, moved, stayed = [], zero, zero
    for l in range(LANE_BITS):
        key_lane.append(jnp.where(used[l] == 1, moved + 16, stayed))
        moved, stayed = moved + used[l], stayed + (one - used[l])
    key_new, moved, stayed = [], zero, zero
    for k in range(LANE_BITS):
        from_row = jnp.where(order[k] >= LANE_BITS, one, zero)
        key_new.append(jnp.where(from_row == 1, moved + 16, stayed))
        moved, stayed = moved + from_row, stayed + (one - from_row)
    match = []
    for l in range(LANE_BITS):
        total = zero
        for k in range(LANE_BITS):
            total = total + jnp.where(key_lane[l] == key_new[k], order[k] + 16 * k, zero)
        match.append(total)
    new_in_lane = [m >> 4 for m in match]
    lane_before, row_before = [], [None] * ROW_BITS
    middle_before = zero
    for l in range(LANE_BITS):
        r = row_of_lane[l]
        old = match[l] & 15
        at_spare = crosses_middle * jnp.where(spare == l, one, zero)
        lane_before.append(jnp.where(crosses[r] == 1, wanted[r], jnp.where(at_spare == 1, wanted[middle], old)))
        row_before[r] = jnp.where(crosses[r] == 1, old, wanted[r]) & 7
        middle_before = middle_before + at_spare * old
    row_before[middle] = jnp.where(crosses_middle == 1, middle_before, wanted[middle]) & 7
    slots = [r if r < middle else r - 1 for r in range(ROW_BITS)]
    slots[middle] = spare
    return crosses, wanted, slots, row_before, lane_before, new_in_lane


def middle_high(plan):
    crosses, wanted, slots, row_before = plan
    place = jnp.int32(3)
    for r in range(3):
        place = jnp.where(row_before[r] == LANE_BITS, r, place)

    def exchanged(values):
        values = [jnp.int32(value) for value in values]
        moved = values[3]
        for r in range(3):
            moved = jnp.where(place == r, values[r], moved)
        return [jnp.where(place == r, values[3], values[r]) for r in range(3)] + [moved] + values[4:]

    return *(exchanged(values) for values in (crosses, wanted, slots, row_before)), place


def moved_bits(index, sources, targets):
    total = jnp.zeros_like(index)
    for source, target in zip(sources, targets, strict=True):
        total = total | (((index >> source) & 1) << target)
    return total


def one_hot(count, index):
    rows = lax.broadcasted_iota(jnp.int32, (count, index.shape[1]), 0)
    return jnp.where(rows == index, 1.0, 0.0).astype(F32).astype(BF16)


def crossed(values, before, after, index):
    values = list(values)

    def butterfly(masks):
        for bit, mask in enumerate(masks):
            for i in range(len(values)):
                if not i >> bit & 1:
                    low, high = values[i], values[i | 1 << bit]
                    values[i] = jnp.where(mask, high, low)
                    values[i | 1 << bit] = jnp.where(mask, low, high)

    butterfly(before)
    for i, lanes in enumerate(index):
        values[i] = jnp.take_along_axis(values[i], lanes, axis=1, mode="promise_in_bounds")
    butterfly(after)
    return values


def masks_of(lane, crosses, bits):
    return [((lane >> bit) & 1) * cross == 1 for cross, bit in zip(crosses, bits, strict=True)]


def lanes_of(lane, crosses, bits):
    moves = [cross << bit for cross, bit in zip(crosses, bits, strict=True)]
    offsets = [jnp.int32(0)]
    for move in moves:
        offsets += [offset | move for offset in offsets]
    return [jnp.bitwise_xor(lane, offset) for offset in offsets]


def first_kernel(lo_bits, order_hbm, x_hbm, gates_hbm, *refs):
    outs, (order_ref, x_ref, gates_ref, work, sems) = refs[:-5], refs[-5:]
    outs, orders_out = outs[:-1], outs[-1]
    parts = 1 << lo_bits
    fetches = [
        pltpu.make_async_copy(order_hbm, order_ref, sems.at[0]),
        pltpu.make_async_copy(gates_hbm.at[pl.ds(0, 2)], gates_ref, sems.at[1]),
        pltpu.make_async_copy(x_hbm, x_ref, sems.at[2]),
    ]
    for fetch in fetches:
        fetch.start()
    fetches[0].wait()
    order = [order_ref[k] for k in range(LANE_BITS + ROW_BITS)]
    *plan, lane_before, new_in_lane = plan_of(order, lo_bits)
    folded = lo_bits + 3 < LANE_BITS
    place = jnp.int32(3)
    if folded:
        *plan, place = middle_high(plan)
    crosses, wanted, slots, row_before = plan
    lane = lax.broadcasted_iota(jnp.int32, (8, WIDTH), 1)
    orders_out[0] = moved_bits(lane, range(LANE_BITS), new_in_lane)
    turn = [jnp.where(place == r, 3, r) for r in range(3)] + [place] + [*range(4, LANE_BITS)]
    orders_out[1] = moved_bits(lane, range(LANE_BITS), turn)
    if folded:
        middle = jnp.int32(0)
        for r in range(ROW_BITS):
            middle = jnp.where(row_before[r] == LANE_BITS, r, middle)
        after_middle = [jnp.where(middle < r, 1, 0) for r in range(ROW_BITS)]
        index = lax.broadcasted_iota(jnp.int32, (1, WIDTH), 1)
        rows = one_hot(WIDTH, moved_bits(index, row_before, [r - after_middle[r] for r in range(ROW_BITS)]))
        offsets = [jnp.int32(0)]
        for r in range(3, ROW_BITS):
            stride = jnp.where(middle == r, WIDTH, jnp.left_shift(1, r - after_middle[r]))
            offsets += [offset + stride for offset in offsets]
    else:
        index = lax.broadcasted_iota(jnp.int32, (1, 2 * WIDTH), 1)
        rows = one_hot(2 * WIDTH, moved_bits(index, row_before, range(ROW_BITS)))
    old_lane = moved_bits(lane, range(LANE_BITS), lane_before)
    fetches[1].wait()
    fetches[2].wait()
    real, imag = halves(gates_ref[0, 0]), halves(gates_ref[0, 1])
    if folded:
        both = [dot(rows, jnp.concatenate([real[i], imag[i]], axis=1)).astype(BF16) for i in range(2)]
        real, imag = [[half[:, c * WIDTH : (c + 1) * WIDTH] for half in both] for c in range(2)]
    matrix0 = [block_matrix(real[i], imag[i]) for i in range(2)]
    real, imag = halves(gates_ref[1, 0]), halves(gates_ref[1, 1])
    matrix1 = [block_matrix(real[i], imag[i]) for i in range(2)]
    pieces = [[x_ref[pl.ds(m * 2 + c, WIDTH, stride=4), :] for m in range(2)] for c in range(2)]
    state = jnp.concatenate([jnp.concatenate(row, axis=1) for row in pieces], axis=0)
    state = dot3(matrix0, halves(state))
    if folded:
        for c in range(2):
            for m in range(2):
                work[c, m * WIDTH : (m + 1) * WIDTH] = state[c * WIDTH : (c + 1) * WIDTH, m * WIDTH : (m + 1) * WIDTH]
        state = halves(
            jnp.concatenate(
                [
                    jnp.concatenate([work[c, pl.ds(pl.multiple_of(offset, 8), 8), :] for offset in offsets], axis=0)
                    for c in range(2)
                ],
                axis=1,
            )
        )
    else:
        state = [dot(rows, half).astype(BF16) for half in halves(turned(state))]
    state = dot3(state, matrix1, transposed=True)
    before, after = masks_of(lane, crosses[3:], wanted[3:]), masks_of(lane, crosses[3:], slots[3:])
    index = lanes_of(old_lane, crosses[3:], wanted[3:])
    for c in range(2):
        values = [state[8 * v : 8 * v + 8, c * WIDTH : (c + 1) * WIDTH] for v in range(32)]
        for v, value in enumerate(crossed(values, before, after, index)):
            work[c, pl.ds(8 * v, 8), :] = value
    masks = masks_of(lane, crosses[:3], slots[:3])
    index = lanes_of(lane, crosses[:3], slots[:3])
    for c in range(2):
        for group in range(4):
            places = [pl.ds(group * 64 + o, 8, stride=8) for o in range(8)]
            values = crossed([work[c, place, :] for place in places], masks, masks, index)
            for place, value in zip(places, values, strict=True):
                work[c, place, :] = value
    me = lax.axis_index("lo")
    count = 2 * WIDTH // parts
    near = outs[0].shape[0]
    for step in range(parts):
        out = outs[0].at[step] if step < near else outs[1 + step - near]
        source = pl.multiple_of(jnp.bitwise_xor(me, step) * count, 8)
        for c in range(2):
            out[c] = work[c, pl.ds(source, count), :]


def turned(value):
    return jnp.concatenate(
        [
            jnp.concatenate([value[i * WIDTH : (i + 1) * WIDTH, j * WIDTH : (j + 1) * WIDTH] for i in range(2)], axis=1)
            for j in range(2)
        ],
        axis=0,
    )


def mixed(coefs_ref, own, other):
    own_r, own_i, other_r, other_i = [jnp.concatenate([coefs_ref[i]] * (own.shape[-2] // 8), axis=0) for i in range(4)]
    return (
        own_r * own[0] - own_i * own[1] + (other_r * other[0] - other_i * other[1]),
        own_r * own[1] + own_i * own[0] + (other_r * other[1] + other_i * other[0]),
    )


def mix_kernel(coefs_ref, matrix_ref, own_ref, other_ref, *outs):
    values = [mixed(coefs_ref, own_ref.at[k + 1], other_ref.at[k + 1]) for k in range(len(outs))]
    for out_ref, value in zip(outs, low_gate(matrix_ref, values), strict=True):
        out_ref[0], out_ref[1] = value


def arrival(parts):
    near = parts // 2
    return [0, *range(near, parts - 1)], [*range(1, near), parts - 1]


def low_weights_kernel(orders_ref, gate_hbm, gates_hbm, out_ref, coefs_out, mats_ref, gate_ref, sems):
    fetches = [
        pltpu.make_async_copy(gates_hbm.at[3], mats_ref, sems.at[0]),
        pltpu.make_async_copy(gate_hbm, gate_ref, sems.at[1]),
    ]
    for fetch in fetches:
        fetch.start()
    lanes = one_hot(WIDTH, orders_ref[0, 0:1])
    for fetch in fetches:
        fetch.wait()
    side = jnp.right_shift(lax.axis_index("hi"), lax.axis_size("hi").bit_length() - 2) & 1
    for other in range(2):
        for c in range(2):
            coefs_out[2 * other + c] = jnp.full((8, WIDTH), gate_ref[c, side, side ^ other])
    for i in range(2):
        real, imag = [dot(halves(mats_ref[c])[i], lanes).T for c in range(2)]
        out_ref[i] = block_matrix(real, -imag).astype(BF16)


def high_weights_kernel(lo_bits, orders_ref, gates_hbm, early_ref, late_ref, gates_ref, sems):
    fetches = [pltpu.make_async_copy(gates_hbm.at[2 + 2 * g], gates_ref.at[g], sems.at[g]) for g in range(2)]
    for fetch in fetches:
        fetch.start()
    parts = 1 << lo_bits
    kept = WIDTH // parts
    me = lax.axis_index("lo")
    index = lax.broadcasted_iota(jnp.int32, (1, WIDTH), 1)
    source = orders_ref[1, 0:1] % kept
    early, late = arrival(parts)
    for place, step in enumerate(early + late):
        source = source + jnp.where(index // kept == place, jnp.bitwise_xor(me, step) * kept, 0)
    rows = one_hot(WIDTH, source)
    for fetch in fetches:
        fetch.wait()

    def exact(left, right):
        return lax.dot_general(
            left, right, (((1,), (0,)), ((), ())), precision=lax.Precision.HIGHEST, preferred_element_type=F32
        )

    first, last = [[gates_ref[g, c] for c in range(2)] for g in range(2)]
    real = halves(exact(last[0], first[0]) - exact(last[1], first[1]))
    imag = halves(exact(last[0], first[1]) + exact(last[1], first[0]))
    half = len(early) * kept
    for i in range(2):
        both = [dot(part[i], rows) for part in (real, imag)]
        early_ref[i] = block_matrix(*[part[:, :half] for part in both]).astype(BF16)
        late_ref[i] = block_matrix(*[part[:, half:] for part in both]).astype(BF16)


def low_gate(matrix_ref, values):
    state = jnp.concatenate([jnp.concatenate(value, axis=1) for value in values], axis=0)
    state = dot3(halves(state), (matrix_ref[0], matrix_ref[1]))
    count = state.shape[0] // len(values)
    return [
        [state[i * count : (i + 1) * count, c * WIDTH : (c + 1) * WIDTH] for c in range(2)] for i in range(len(values))
    ]


def for_high(values):
    kept = values[0][0].shape[0] // 2
    return jnp.concatenate(
        [
            jnp.concatenate([value[c][m * kept : (m + 1) * kept] for m in range(2)], axis=1)
            for c in range(2)
            for value in values
        ],
        axis=0,
    )


def copy_kernel(in_ref, out_ref):
    out_ref[...] = in_ref[...]


def low_kernel(matrix_ref, in_ref, out_ref):
    (value,) = low_gate(matrix_ref, [(in_ref[0], in_ref[1])])
    out_ref[0], out_ref[1] = value


def early_kernel(coefs_ref, low_gate_ref, high_gate_ref, near_own_ref, near_other_ref, *refs):
    ins, out_ref = refs[:-1], refs[-1]
    values = [mixed(coefs_ref, near_own_ref.at[0], near_other_ref.at[0])]
    values += [mixed(coefs_ref, own, other) for own, other in zip(ins[0::2], ins[1::2], strict=True)]
    out_ref[...] = dot3((high_gate_ref[0], high_gate_ref[1]), halves(for_high(low_gate(low_gate_ref, values))))


def last_kernel(coefs_ref, high_gate_ref, early_ref, own_ref, other_ref, *refs):
    ins, (out_hbm, out_ref, sems) = refs[:-3], refs[-3:]
    values = [(ref[0], ref[1]) for ref in ins] + [mixed(coefs_ref, own_ref, other_ref)]
    high, low = halves(for_high(values))
    state = jnp.concatenate([low, high, high], axis=0)
    sends = []
    half = WIDTH // 2
    for i in range(2):
        matrix = [
            jnp.concatenate(
                [high_gate_ref[j, c * WIDTH + i * half : c * WIDTH + (i + 1) * half] for c in range(2)], axis=0
            )
            for j in (0, 1, 0)
        ]
        result = dot(jnp.concatenate(matrix, axis=1), state)
        for c in range(2):
            for m in range(2):
                at = c * WIDTH + i * half
                out_ref[pl.ds(i * 256 + m * 2 + c, half, stride=4), :] = (
                    early_ref[at : at + half, m * WIDTH : (m + 1) * WIDTH]
                    + result[c * half : (c + 1) * half, m * WIDTH : (m + 1) * WIDTH]
                )
        sends.append(
            pltpu.make_async_copy(out_ref.at[pl.ds(i * 256, 256)], out_hbm.at[pl.ds(i * 256, 256)], sems.at[i])
        )
        sends[-1].start()
    for send in sends:
        send.wait()


def swapped(block, axis, distance):
    count = lax.axis_size(axis)
    return lax.ppermute(block, axis, [(i, i ^ distance) for i in range(count)])


PARAMS = pltpu.CompilerParams(vmem_limit_bytes=8 << 20)
HBM = pl.BlockSpec(memory_space=pltpu.HBM)
VMEM = pl.BlockSpec(memory_space=pltpu.VMEM)


def in_hbm(value):
    return pltpu.with_memory_space_constraint(value, pltpu.HBM)


def on_device(amplitudes, gate_mats, dev_gate, qubit_order):
    parts = lax.axis_size("lo")
    lo_bits = parts.bit_length() - 1
    top = lax.axis_size("hi") // 2
    kept = WIDTH // parts
    rows = amplitudes.reshape(2, 256, WIDTH).transpose(1, 0, 2).reshape(512, WIDTH)
    block = pltpu.VMEM((2, 2 * kept, WIDTH), F32)
    near = parts // 2
    near_own, *far_own, orders = pl.pallas_call(
        functools.partial(first_kernel, lo_bits),
        out_shape=[pltpu.VMEM((near, 2, 2 * kept, WIDTH), F32)]
        + [block] * (parts - near)
        + [pltpu.VMEM((2, 8, WIDTH), jnp.int32)],
        in_specs=[HBM] * 3,
        out_specs=[VMEM] * (parts - near + 2),
        scratch_shapes=[
            pltpu.SMEM((LANE_BITS + ROW_BITS,), jnp.int32),
            pltpu.VMEM((512, WIDTH), F32),
            pltpu.VMEM((2, 2, WIDTH, WIDTH), F32),
            pltpu.VMEM((2, 256, WIDTH), F32),
            pltpu.SemaphoreType.DMA((3,)),
        ],
        compiler_params=PARAMS,
        name="first_gates",
    )(in_hbm(qubit_order), in_hbm(rows), in_hbm(gate_mats))
    near_other = swapped(near_own, "hi", top)
    far_own = [swapped(far, "lo", near + i) for i, far in enumerate(far_own)]
    counts = [2 * kept * len(steps) for steps in arrival(parts)]
    low_weights, coefs = pl.pallas_call(
        low_weights_kernel,
        out_shape=[pltpu.VMEM((2, 256, 256), BF16), pltpu.VMEM((4, 8, WIDTH), F32)],
        in_specs=[VMEM, HBM, HBM],
        out_specs=[VMEM] * 2,
        scratch_shapes=[pltpu.VMEM((2, WIDTH, WIDTH), F32), pltpu.SMEM((2, 2, 2), F32), pltpu.SemaphoreType.DMA((2,))],
        compiler_params=PARAMS,
        name="low_weights",
    )(orders, in_hbm(dev_gate), in_hbm(gate_mats))
    early_weights, late_weights = pl.pallas_call(
        functools.partial(high_weights_kernel, lo_bits),
        out_shape=[pltpu.VMEM((2, 256, count), BF16) for count in counts],
        in_specs=[VMEM, HBM],
        out_specs=[VMEM] * 2,
        scratch_shapes=[pltpu.VMEM((2, 2, WIDTH, WIDTH), F32), pltpu.SemaphoreType.DMA((2,))],
        compiler_params=PARAMS,
        name="high_weights",
    )(orders, in_hbm(gate_mats))
    far_own[-1] = pl.pallas_call(
        low_kernel, out_shape=block, in_specs=[VMEM] * 2, out_specs=VMEM, compiler_params=PARAMS, name="low_gate"
    )(low_weights, far_own[-1])
    far_other = [swapped(far, "hi", top) for far in far_own]
    far_other[0] = pl.pallas_call(
        copy_kernel, out_shape=block, in_specs=[VMEM], out_specs=VMEM, compiler_params=PARAMS, name="arrived"
    )(far_other[0])
    mixes = pl.pallas_call(
        mix_kernel,
        out_shape=[block] * (near - 1),
        in_specs=[VMEM] * 4,
        out_specs=[VMEM] * (near - 1),
        compiler_params=PARAMS,
        name="mix_pair",
    )(coefs, low_weights, near_own, near_other)
    mixes = [swapped(mix, "lo", 1 + i) for i, mix in enumerate(mixes)]
    pairs = [value for pair in zip(far_own[:-1], far_other[:-1], strict=True) for value in pair]
    early = pl.pallas_call(
        early_kernel,
        out_shape=pltpu.VMEM((256, 256), F32),
        in_specs=[VMEM] * (5 + len(pairs)),
        out_specs=VMEM,
        compiler_params=PARAMS,
        name="early_gate",
    )(coefs, low_weights, early_weights, near_own, near_other, *pairs)
    out = pl.pallas_call(
        last_kernel,
        out_shape=jax.ShapeDtypeStruct((512, WIDTH), F32),
        in_specs=[VMEM] * (5 + len(mixes)),
        out_specs=HBM,
        scratch_shapes=[pltpu.VMEM((512, WIDTH), F32), pltpu.SemaphoreType.DMA((2,))],
        compiler_params=PARAMS,
        name="last_gates",
    )(coefs, late_weights, early, far_own[-1], far_other[-1], *mixes)
    return out.reshape(256, 2, WIDTH).transpose(1, 0, 2).reshape(2, -1)


def solution(mesh):
    return jax.shard_map(
        on_device,
        mesh=mesh,
        in_specs=(P(None, ("hi", "lo")), P(), P(), P()),
        out_specs=P(None, ("hi", "lo")),
        check_vma=False,
    )
```

```python
import functools

import jax
import jax.numpy as jnp
from jax import lax
from jax.experimental import pallas as pl
from jax.experimental.pallas import tpu as pltpu
from jax.sharding import PartitionSpec as P

WIDTH = 128
LANE_BITS = 7
ROW_BITS = 8
F32, BF16 = jnp.float32, jnp.bfloat16


def halves(value):
    high = value.astype(BF16)
    return high, (value - high.astype(F32)).astype(BF16)


def dot(left, right, transposed=False):
    return lax.dot_general(
        left, right, (((1,), (1 if transposed else 0,)), ((), ())), preferred_element_type=F32
    )


def dot3(left, right, transposed=False):
    (lh, ll), (rh, rl) = left, right
    return dot(lh, rl, transposed) + dot(ll, rh, transposed) + dot(lh, rh, transposed)


def block_matrix(real, imag):
    return jnp.concatenate(
        [jnp.concatenate([real, -imag], axis=1), jnp.concatenate([imag, real], axis=1)], axis=0
    )


def new_positions(lo_bits):
    kept = LANE_BITS - lo_bits
    return [8 + r for r in range(kept)] + [7] + [8 + r for r in range(kept, LANE_BITS)]


def plan_of(order, lo_bits):
    one, zero = jnp.int32(1), jnp.int32(0)
    middle = LANE_BITS - lo_bits
    row_of_lane = [l if l < middle else l + 1 for l in range(LANE_BITS)]
    wanted = [order[k] for k in new_positions(lo_bits)]
    crosses = [jnp.where(w < LANE_BITS, one, zero) for w in wanted]
    crosses_middle = crosses[middle]
    used, before = [], zero
    spare = zero
    for l in range(LANE_BITS):
        free = (one - crosses[row_of_lane[l]]) * crosses_middle * jnp.where(before == 0, one, zero)
        spare = spare + free * l
        used.append(crosses[row_of_lane[l]] + free)
        before = before + free
    key_lane, moved, stayed = [], zero, zero
    for l in range(LANE_BITS):
        key_lane.append(jnp.where(used[l] == 1, moved + 16, stayed))
        moved, stayed = moved + used[l], stayed + (one - used[l])
    key_new, moved, stayed = [], zero, zero
    for k in range(LANE_BITS):
        from_row = jnp.where(order[k] >= LANE_BITS, one, zero)
        key_new.append(jnp.where(from_row == 1, moved + 16, stayed))
        moved, stayed = moved + from_row, stayed + (one - from_row)
    match = []
    for l in range(LANE_BITS):
        total = zero
        for k in range(LANE_BITS):
            total = total + jnp.where(key_lane[l] == key_new[k], order[k] + 16 * k, zero)
        match.append(total)
    new_in_lane = [m >> 4 for m in match]
    lane_before, row_before = [], [None] * ROW_BITS
    middle_before = zero
    for l in range(LANE_BITS):
        r = row_of_lane[l]
        old = match[l] & 15
        at_spare = crosses_middle * jnp.where(spare == l, one, zero)
        lane_before.append(jnp.where(crosses[r] == 1, wanted[r], jnp.where(at_spare == 1, wanted[middle], old)))
        row_before[r] = jnp.where(crosses[r] == 1, old, wanted[r]) & 7
        middle_before = middle_before + at_spare * old
    row_before[middle] = jnp.where(crosses_middle == 1, middle_before, wanted[middle]) & 7
    slots = [r if r < middle else r - 1 for r in range(ROW_BITS)]
    slots[middle] = spare
    return crosses, wanted, slots, row_before, lane_before, new_in_lane


def middle_high(plan):
    crosses, wanted, slots, row_before = plan
    place = jnp.int32(3)
    for r in range(3):
        place = jnp.where(row_before[r] == LANE_BITS, r, place)

    def exchanged(values):
        values = [jnp.int32(value) for value in values]
        moved = values[3]
        for r in range(3):
            moved = jnp.where(place == r, values[r], moved)
        return [jnp.where(place == r, values[3], values[r]) for r in range(3)] + [moved] + values[4:]

    return *(exchanged(values) for values in (crosses, wanted, slots, row_before)), place


def moved_bits(index, sources, targets):
    total = jnp.zeros_like(index)
    for source, target in zip(sources, targets, strict=True):
        total = total | (((index >> source) & 1) << target)
    return total


def one_hot(count, index):
    rows = lax.broadcasted_iota(jnp.int32, (count, index.shape[1]), 0)
    return jnp.where(rows == index, 1.0, 0.0).astype(F32).astype(BF16)


def crossed(values, before, after, index):
    values = list(values)

    def butterfly(masks):
        for bit, mask in enumerate(masks):
            for i in range(len(values)):
                if not i >> bit & 1:
                    low, high = values[i], values[i | 1 << bit]
                    values[i] = jnp.where(mask, high, low)
                    values[i | 1 << bit] = jnp.where(mask, low, high)

    butterfly(before)
    for i, lanes in enumerate(index):
        if lanes is None:
            continue
        values[i] = jnp.take_along_axis(values[i], lanes, axis=1, mode="promise_in_bounds")
    butterfly(after)
    return values


def masks_of(lane, crosses, bits):
    return [((lane >> bit) & 1) * cross == 1 for cross, bit in zip(crosses, bits, strict=True)]


def lanes_of(lane, crosses, bits):
    moves = [cross << bit for cross, bit in zip(crosses, bits, strict=True)]
    offsets = [jnp.int32(0)]
    for move in moves:
        offsets += [offset | move for offset in offsets]
    return [jnp.bitwise_xor(lane, offset) for offset in offsets]


def first_kernel(lo_bits, order_hbm, x_hbm, gates_hbm, *refs):
    outs, (order_ref, x_ref, gates_ref, work, sems) = refs[:-5], refs[-5:]
    outs, orders_out = outs[:-1], outs[-1]
    parts = 1 << lo_bits
    fetches = [
        pltpu.make_async_copy(order_hbm, order_ref, sems.at[0]),
        pltpu.make_async_copy(gates_hbm.at[pl.ds(0, 2)], gates_ref, sems.at[1]),
        pltpu.make_async_copy(x_hbm, x_ref, sems.at[2]),
    ]
    for fetch in fetches:
        fetch.start()
    fetches[0].wait()
    order = [order_ref[k] for k in range(LANE_BITS + ROW_BITS)]
    *plan, lane_before, new_in_lane = plan_of(order, lo_bits)
    folded = lo_bits + 3 < LANE_BITS
    place = jnp.int32(3)
    if folded:
        *plan, place = middle_high(plan)
    crosses, wanted, slots, row_before = plan
    lane = lax.broadcasted_iota(jnp.int32, (8, WIDTH), 1)
    orders_out[0] = moved_bits(lane, range(LANE_BITS), new_in_lane)
    turn = [jnp.where(place == r, 3, r) for r in range(3)] + [place] + [*range(4, LANE_BITS)]
    orders_out[1] = moved_bits(lane, range(LANE_BITS), turn)
    if folded:
        middle = jnp.int32(0)
        for r in range(ROW_BITS):
            middle = jnp.where(row_before[r] == LANE_BITS, r, middle)
        after_middle = [jnp.where(middle < r, 1, 0) for r in range(ROW_BITS)]
        index = lax.broadcasted_iota(jnp.int32, (1, WIDTH), 1)
        rows = one_hot(WIDTH, moved_bits(index, row_before, [r - after_middle[r] for r in range(ROW_BITS)]))
        offsets = [jnp.int32(0)]
        for r in range(3, ROW_BITS):
            stride = jnp.where(middle == r, WIDTH, jnp.left_shift(1, r - after_middle[r]))
            offsets += [offset + stride for offset in offsets]
    else:
        index = lax.broadcasted_iota(jnp.int32, (1, 2 * WIDTH), 1)
        rows = one_hot(2 * WIDTH, moved_bits(index, row_before, range(ROW_BITS)))
    old_lane = moved_bits(lane, range(LANE_BITS), lane_before)
    fetches[1].wait()
    fetches[2].wait()
    real, imag = halves(gates_ref[0, 0]), halves(gates_ref[0, 1])
    if folded:
        both = [dot(rows, jnp.concatenate([real[i], imag[i]], axis=1)).astype(BF16) for i in range(2)]
        real, imag = [[half[:, c * WIDTH : (c + 1) * WIDTH] for half in both] for c in range(2)]
    matrix0 = [block_matrix(real[i], imag[i]) for i in range(2)]
    real, imag = halves(gates_ref[1, 0]), halves(gates_ref[1, 1])
    matrix1 = [block_matrix(real[i], imag[i]) for i in range(2)]
    pieces = [[x_ref[pl.ds(m * 2 + c, WIDTH, stride=4), :] for m in range(2)] for c in range(2)]
    state = jnp.concatenate([jnp.concatenate(row, axis=1) for row in pieces], axis=0)
    state = dot3(matrix0, halves(state))
    if folded:
        for c in range(2):
            for m in range(2):
                work[c, m * WIDTH : (m + 1) * WIDTH] = state[c * WIDTH : (c + 1) * WIDTH, m * WIDTH : (m + 1) * WIDTH]
        state = halves(
            jnp.concatenate(
                [
                    jnp.concatenate([work[c, pl.ds(pl.multiple_of(offset, 8), 8), :] for offset in offsets], axis=0)
                    for c in range(2)
                ],
                axis=1,
            )
        )
    else:
        state = [dot(rows, half).astype(BF16) for half in halves(turned(state))]
    state = dot3(state, matrix1, transposed=True)
    before, after = masks_of(lane, crosses[3:], wanted[3:]), masks_of(lane, crosses[3:], slots[3:])
    index = lanes_of(old_lane, crosses[3:], wanted[3:])
    for c in range(2):
        values = [state[8 * v : 8 * v + 8, c * WIDTH : (c + 1) * WIDTH] for v in range(32)]
        for v, value in enumerate(crossed(values, before, after, index)):
            work[c, pl.ds(8 * v, 8), :] = value
    masks = masks_of(lane, crosses[:3], slots[:3])
    index = [None] + lanes_of(lane, crosses[:3], slots[:3])[1:]
    for c in range(2):
        for group in range(4):
            places = [pl.ds(group * 64 + o, 8, stride=8) for o in range(8)]
            values = crossed([work[c, place, :] for place in places], masks, masks, index)
            for place, value in zip(places, values, strict=True):
                work[c, place, :] = value
    me = lax.axis_index("lo")
    count = 2 * WIDTH // parts
    near = outs[0].shape[0]
    for step in range(parts):
        out = outs[0].at[step] if step < near else outs[1 + step - near]
        source = pl.multiple_of(jnp.bitwise_xor(me, step) * count, 8)
        for c in range(2):
            out[c] = work[c, pl.ds(source, count), :]


def turned(value):
    return jnp.concatenate(
        [
            jnp.concatenate([value[i * WIDTH : (i + 1) * WIDTH, j * WIDTH : (j + 1) * WIDTH] for i in range(2)], axis=1)
            for j in range(2)
        ],
        axis=0,
    )


def mixed(coefs_ref, own, other):
    own_r, own_i, other_r, other_i = [jnp.concatenate([coefs_ref[i]] * (own.shape[-2] // 8), axis=0) for i in range(4)]
    return (
        own_r * own[0] - own_i * own[1] + (other_r * other[0] - other_i * other[1]),
        own_r * own[1] + own_i * own[0] + (other_r * other[1] + other_i * other[0]),
    )


def mix_kernel(coefs_ref, matrix_ref, own_ref, other_ref, *outs):
    values = [mixed(coefs_ref, own_ref.at[k + 1], other_ref.at[k + 1]) for k in range(len(outs))]
    for out_ref, value in zip(outs, low_gate(matrix_ref, values), strict=True):
        out_ref[0], out_ref[1] = value


def arrival(parts):
    near = parts // 2
    return [0, *range(near, parts - 1)], [*range(1, near), parts - 1]


def low_weights_kernel(orders_ref, gate_hbm, gates_hbm, out_ref, coefs_out, mats_ref, gate_ref, sems):
    fetches = [
        pltpu.make_async_copy(gates_hbm.at[3], mats_ref, sems.at[0]),
        pltpu.make_async_copy(gate_hbm, gate_ref, sems.at[1]),
    ]
    for fetch in fetches:
        fetch.start()
    lanes = one_hot(WIDTH, orders_ref[0, 0:1])
    for fetch in fetches:
        fetch.wait()
    side = jnp.right_shift(lax.axis_index("hi"), lax.axis_size("hi").bit_length() - 2) & 1
    for other in range(2):
        for c in range(2):
            coefs_out[2 * other + c] = jnp.full((8, WIDTH), gate_ref[c, side, side ^ other])
    for i in range(2):
        real, imag = [dot(halves(mats_ref[c])[i], lanes).T for c in range(2)]
        out_ref[i] = block_matrix(real, -imag).astype(BF16)


def high_weights_kernel(lo_bits, orders_ref, gates_hbm, early_ref, late_ref, gates_ref, sems):
    fetches = [pltpu.make_async_copy(gates_hbm.at[2 + 2 * g], gates_ref.at[g], sems.at[g]) for g in range(2)]
    for fetch in fetches:
        fetch.start()
    parts = 1 << lo_bits
    kept = WIDTH // parts
    me = lax.axis_index("lo")
    index = lax.broadcasted_iota(jnp.int32, (1, WIDTH), 1)
    source = orders_ref[1, 0:1] % kept
    early, late = arrival(parts)
    for place, step in enumerate(early + late):
        source = source + jnp.where(index // kept == place, jnp.bitwise_xor(me, step) * kept, 0)
    rows = one_hot(WIDTH, source)
    for fetch in fetches:
        fetch.wait()

    def exact(left, right):
        return lax.dot_general(
            left, right, (((1,), (0,)), ((), ())), precision=lax.Precision.HIGHEST, preferred_element_type=F32
        )

    first, last = [[gates_ref[g, c] for c in range(2)] for g in range(2)]
    real = halves(exact(last[0], first[0]) - exact(last[1], first[1]))
    imag = halves(exact(last[0], first[1]) + exact(last[1], first[0]))
    half = len(early) * kept
    for i in range(2):
        both = [dot(part[i], rows) for part in (real, imag)]
        early_ref[i] = block_matrix(*[part[:, :half] for part in both]).astype(BF16)
        late_ref[i] = block_matrix(*[part[:, half:] for part in both]).astype(BF16)


def low_gate(matrix_ref, values):
    state = jnp.concatenate([jnp.concatenate(value, axis=1) for value in values], axis=0)
    state = dot3(halves(state), (matrix_ref[0], matrix_ref[1]))
    count = state.shape[0] // len(values)
    return [
        [state[i * count : (i + 1) * count, c * WIDTH : (c + 1) * WIDTH] for c in range(2)] for i in range(len(values))
    ]


def for_high(values):
    kept = values[0][0].shape[0] // 2
    return jnp.concatenate(
        [
            jnp.concatenate([value[c][m * kept : (m + 1) * kept] for m in range(2)], axis=1)
            for c in range(2)
            for value in values
        ],
        axis=0,
    )


def copy_kernel(in_ref, out_ref):
    out_ref[...] = in_ref[...]


def low_kernel(matrix_ref, in_ref, out_ref):
    (value,) = low_gate(matrix_ref, [(in_ref[0], in_ref[1])])
    out_ref[0], out_ref[1] = value


def early_kernel(coefs_ref, low_gate_ref, high_gate_ref, near_own_ref, near_other_ref, *refs):
    ins, out_ref = refs[:-1], refs[-1]
    values = [mixed(coefs_ref, near_own_ref.at[0], near_other_ref.at[0])]
    values += [mixed(coefs_ref, own, other) for own, other in zip(ins[0::2], ins[1::2], strict=True)]
    out_ref[...] = dot3((high_gate_ref[0], high_gate_ref[1]), halves(for_high(low_gate(low_gate_ref, values))))


def last_kernel(coefs_ref, high_gate_ref, early_ref, own_ref, other_ref, *refs):
    ins, (out_hbm, out_ref, sems) = refs[:-3], refs[-3:]
    values = [(ref[0], ref[1]) for ref in ins] + [mixed(coefs_ref, own_ref, other_ref)]
    high, low = halves(for_high(values))
    state = jnp.concatenate([low, high, high], axis=0)
    sends = []
    half = WIDTH // 4
    for i in range(4):
        matrix = [
            jnp.concatenate(
                [high_gate_ref[j, c * WIDTH + i * half : c * WIDTH + (i + 1) * half] for c in range(2)], axis=0
            )
            for j in (0, 1, 0)
        ]
        result = dot(jnp.concatenate(matrix, axis=1), state)
        for c in range(2):
            for m in range(2):
                at = c * WIDTH + i * half
                out_ref[pl.ds(i * 128 + m * 2 + c, half, stride=4), :] = (
                    early_ref[at : at + half, m * WIDTH : (m + 1) * WIDTH]
                    + result[c * half : (c + 1) * half, m * WIDTH : (m + 1) * WIDTH]
                )
        sends.append(
            pltpu.make_async_copy(out_ref.at[pl.ds(i * 128, 128)], out_hbm.at[pl.ds(i * 128, 128)], sems.at[i])
        )
        sends[-1].start()
    for send in sends:
        send.wait()


def swapped(block, axis, distance):
    count = lax.axis_size(axis)
    return lax.ppermute(block, axis, [(i, i ^ distance) for i in range(count)])


PARAMS = pltpu.CompilerParams(vmem_limit_bytes=8 << 20)
HBM = pl.BlockSpec(memory_space=pltpu.HBM)
VMEM = pl.BlockSpec(memory_space=pltpu.VMEM)


def in_hbm(value):
    return pltpu.with_memory_space_constraint(value, pltpu.HBM)


def on_device(amplitudes, gate_mats, dev_gate, qubit_order):
    parts = lax.axis_size("lo")
    lo_bits = parts.bit_length() - 1
    top = lax.axis_size("hi") // 2
    kept = WIDTH // parts
    rows = amplitudes.reshape(2, 256, WIDTH).transpose(1, 0, 2).reshape(512, WIDTH)
    block = pltpu.VMEM((2, 2 * kept, WIDTH), F32)
    near = parts // 2
    near_own, *far_own, orders = pl.pallas_call(
        functools.partial(first_kernel, lo_bits),
        out_shape=[pltpu.VMEM((near, 2, 2 * kept, WIDTH), F32)]
        + [block] * (parts - near)
        + [pltpu.VMEM((2, 8, WIDTH), jnp.int32)],
        in_specs=[HBM] * 3,
        out_specs=[VMEM] * (parts - near + 2),
        scratch_shapes=[
            pltpu.SMEM((LANE_BITS + ROW_BITS,), jnp.int32),
            pltpu.VMEM((512, WIDTH), F32),
            pltpu.VMEM((2, 2, WIDTH, WIDTH), F32),
            pltpu.VMEM((2, 256, WIDTH), F32),
            pltpu.SemaphoreType.DMA((3,)),
        ],
        compiler_params=PARAMS,
        name="first_gates",
    )(in_hbm(qubit_order), in_hbm(rows), in_hbm(gate_mats))
    near_other = swapped(near_own, "hi", top)
    far_own = [swapped(far, "lo", near + i) for i, far in enumerate(far_own)]
    counts = [2 * kept * len(steps) for steps in arrival(parts)]
    low_weights, coefs = pl.pallas_call(
        low_weights_kernel,
        out_shape=[pltpu.VMEM((2, 256, 256), BF16), pltpu.VMEM((4, 8, WIDTH), F32)],
        in_specs=[VMEM, HBM, HBM],
        out_specs=[VMEM] * 2,
        scratch_shapes=[pltpu.VMEM((2, WIDTH, WIDTH), F32), pltpu.SMEM((2, 2, 2), F32), pltpu.SemaphoreType.DMA((2,))],
        compiler_params=PARAMS,
        name="low_weights",
    )(orders, in_hbm(dev_gate), in_hbm(gate_mats))
    early_weights, late_weights = pl.pallas_call(
        functools.partial(high_weights_kernel, lo_bits),
        out_shape=[pltpu.VMEM((2, 256, count), BF16) for count in counts],
        in_specs=[VMEM, HBM],
        out_specs=[VMEM] * 2,
        scratch_shapes=[pltpu.VMEM((2, 2, WIDTH, WIDTH), F32), pltpu.SemaphoreType.DMA((2,))],
        compiler_params=PARAMS,
        name="high_weights",
    )(orders, in_hbm(gate_mats))
    far_own[-1] = pl.pallas_call(
        low_kernel, out_shape=block, in_specs=[VMEM] * 2, out_specs=VMEM, compiler_params=PARAMS, name="low_gate"
    )(low_weights, far_own[-1])
    far_other = [swapped(far, "hi", top) for far in far_own]
    far_other[0] = pl.pallas_call(
        copy_kernel, out_shape=block, in_specs=[VMEM], out_specs=VMEM, compiler_params=PARAMS, name="arrived"
    )(far_other[0])
    mixes = pl.pallas_call(
        mix_kernel,
        out_shape=[block] * (near - 1),
        in_specs=[VMEM] * 4,
        out_specs=[VMEM] * (near - 1),
        compiler_params=PARAMS,
        name="mix_pair",
    )(coefs, low_weights, near_own, near_other)
    mixes = [swapped(mix, "lo", 1 + i) for i, mix in enumerate(mixes)]
    pairs = [value for pair in zip(far_own[:-1], far_other[:-1], strict=True) for value in pair]
    early = pl.pallas_call(
        early_kernel,
        out_shape=pltpu.VMEM((256, 256), F32),
        in_specs=[VMEM] * (5 + len(pairs)),
        out_specs=VMEM,
        compiler_params=PARAMS,
        name="early_gate",
    )(coefs, low_weights, early_weights, near_own, near_other, *pairs)
    out = pl.pallas_call(
        last_kernel,
        out_shape=jax.ShapeDtypeStruct((512, WIDTH), F32),
        in_specs=[VMEM] * (5 + len(mixes)),
        out_specs=HBM,
        scratch_shapes=[pltpu.VMEM((512, WIDTH), F32), pltpu.SemaphoreType.DMA((4,))],
        compiler_params=PARAMS,
        name="last_gates",
    )(coefs, late_weights, early, far_own[-1], far_other[-1], *mixes)
    return out.reshape(256, 2, WIDTH).transpose(1, 0, 2).reshape(2, -1)


def solution(mesh):
    return jax.shard_map(
        on_device,
        mesh=mesh,
        in_specs=(P(None, ("hi", "lo")), P(), P(), P()),
        out_specs=P(None, ("hi", "lo")),
        check_vma=False,
    )
```

```python
import functools

import jax
import jax.numpy as jnp
from jax import lax
from jax.experimental import pallas as pl
from jax.experimental.pallas import tpu as pltpu
from jax.sharding import PartitionSpec as P

WIDTH = 128
LANE_BITS = 7
ROW_BITS = 8
F32, BF16 = jnp.float32, jnp.bfloat16


def halves(value):
    high = value.astype(BF16)
    return high, (value - high.astype(F32)).astype(BF16)


def dot(left, right, transposed=False):
    return lax.dot_general(
        left, right, (((1,), (1 if transposed else 0,)), ((), ())), preferred_element_type=F32
    )


def dot3(left, right, transposed=False):
    (lh, ll), (rh, rl) = left, right
    return dot(lh, rl, transposed) + dot(ll, rh, transposed) + dot(lh, rh, transposed)


def block_matrix(real, imag):
    return jnp.concatenate(
        [jnp.concatenate([real, -imag], axis=1), jnp.concatenate([imag, real], axis=1)], axis=0
    )


def new_positions(lo_bits):
    kept = LANE_BITS - lo_bits
    return [8 + r for r in range(kept)] + [7] + [8 + r for r in range(kept, LANE_BITS)]


def plan_of(order, lo_bits):
    one, zero = jnp.int32(1), jnp.int32(0)
    middle = LANE_BITS - lo_bits
    row_of_lane = [l if l < middle else l + 1 for l in range(LANE_BITS)]
    wanted = [order[k] for k in new_positions(lo_bits)]
    crosses = [jnp.where(w < LANE_BITS, one, zero) for w in wanted]
    crosses_middle = crosses[middle]
    used, before = [], zero
    spare = zero
    for l in range(LANE_BITS):
        free = (one - crosses[row_of_lane[l]]) * crosses_middle * jnp.where(before == 0, one, zero)
        spare = spare + free * l
        used.append(crosses[row_of_lane[l]] + free)
        before = before + free
    key_lane, moved, stayed = [], zero, zero
    for l in range(LANE_BITS):
        key_lane.append(jnp.where(used[l] == 1, moved + 16, stayed))
        moved, stayed = moved + used[l], stayed + (one - used[l])
    key_new, moved, stayed = [], zero, zero
    for k in range(LANE_BITS):
        from_row = jnp.where(order[k] >= LANE_BITS, one, zero)
        key_new.append(jnp.where(from_row == 1, moved + 16, stayed))
        moved, stayed = moved + from_row, stayed + (one - from_row)
    match = []
    for l in range(LANE_BITS):
        total = zero
        for k in range(LANE_BITS):
            total = total + jnp.where(key_lane[l] == key_new[k], order[k] + 16 * k, zero)
        match.append(total)
    new_in_lane = [m >> 4 for m in match]
    lane_before, row_before = [], [None] * ROW_BITS
    middle_before = zero
    for l in range(LANE_BITS):
        r = row_of_lane[l]
        old = match[l] & 15
        at_spare = crosses_middle * jnp.where(spare == l, one, zero)
        lane_before.append(jnp.where(crosses[r] == 1, wanted[r], jnp.where(at_spare == 1, wanted[middle], old)))
        row_before[r] = jnp.where(crosses[r] == 1, old, wanted[r]) & 7
        middle_before = middle_before + at_spare * old
    row_before[middle] = jnp.where(crosses_middle == 1, middle_before, wanted[middle]) & 7
    slots = [r if r < middle else r - 1 for r in range(ROW_BITS)]
    slots[middle] = spare
    return crosses, wanted, slots, row_before, lane_before, new_in_lane


def middle_high(plan):
    crosses, wanted, slots, row_before = plan
    place = jnp.int32(3)
    for r in range(3):
        place = jnp.where(row_before[r] == LANE_BITS, r, place)

    def exchanged(values):
        values = [jnp.int32(value) for value in values]
        moved = values[3]
        for r in range(3):
            moved = jnp.where(place == r, values[r], moved)
        return [jnp.where(place == r, values[3], values[r]) for r in range(3)] + [moved] + values[4:]

    return *(exchanged(values) for values in (crosses, wanted, slots, row_before)), place


def moved_bits(index, sources, targets):
    total = jnp.zeros_like(index)
    for source, target in zip(sources, targets, strict=True):
        total = total | (((index >> source) & 1) << target)
    return total


def one_hot(count, index):
    rows = lax.broadcasted_iota(jnp.int32, (count, index.shape[1]), 0)
    return jnp.where(rows == index, 1.0, 0.0).astype(F32).astype(BF16)


def crossed(values, before, after, index):
    values = list(values)

    def butterfly(masks):
        for bit, mask in enumerate(masks):
            for i in range(len(values)):
                if not i >> bit & 1:
                    low, high = values[i], values[i | 1 << bit]
                    values[i] = jnp.where(mask, high, low)
                    values[i | 1 << bit] = jnp.where(mask, low, high)

    butterfly(before)
    for i, lanes in enumerate(index):
        if lanes is None:
            continue
        values[i] = jnp.take_along_axis(values[i], lanes, axis=1, mode="promise_in_bounds")
    butterfly(after)
    return values


def masks_of(lane, crosses, bits):
    return [((lane >> bit) & 1) * cross == 1 for cross, bit in zip(crosses, bits, strict=True)]


def lanes_of(lane, crosses, bits):
    moves = [cross << bit for cross, bit in zip(crosses, bits, strict=True)]
    offsets = [jnp.int32(0)]
    for move in moves:
        offsets += [offset | move for offset in offsets]
    return [jnp.bitwise_xor(lane, offset) for offset in offsets]


def first_kernel(lo_bits, order_hbm, x_hbm, gates_hbm, *refs):
    outs, (order_ref, x_ref, gates_ref, work, sems) = refs[:-5], refs[-5:]
    outs, orders_out = outs[:-1], outs[-1]
    parts = 1 << lo_bits
    fetches = [
        pltpu.make_async_copy(order_hbm, order_ref, sems.at[0]),
        pltpu.make_async_copy(gates_hbm.at[pl.ds(0, 2)], gates_ref, sems.at[1]),
        pltpu.make_async_copy(x_hbm, x_ref, sems.at[2]),
    ]
    for fetch in fetches:
        fetch.start()
    fetches[0].wait()
    order = [order_ref[k] for k in range(LANE_BITS + ROW_BITS)]
    *plan, lane_before, new_in_lane = plan_of(order, lo_bits)
    folded = lo_bits + 3 < LANE_BITS
    place = jnp.int32(3)
    if folded:
        *plan, place = middle_high(plan)
    crosses, wanted, slots, row_before = plan
    lane = lax.broadcasted_iota(jnp.int32, (8, WIDTH), 1)
    orders_out[0] = moved_bits(lane, range(LANE_BITS), new_in_lane)
    turn = [jnp.where(place == r, 3, r) for r in range(3)] + [place] + [*range(4, LANE_BITS)]
    orders_out[1] = moved_bits(lane, range(LANE_BITS), turn)
    if folded:
        middle = jnp.int32(0)
        for r in range(ROW_BITS):
            middle = jnp.where(row_before[r] == LANE_BITS, r, middle)
        after_middle = [jnp.where(middle < r, 1, 0) for r in range(ROW_BITS)]
        index = lax.broadcasted_iota(jnp.int32, (1, WIDTH), 1)
        rows = one_hot(WIDTH, moved_bits(index, row_before, [r - after_middle[r] for r in range(ROW_BITS)]))
        offsets = [jnp.int32(0)]
        for r in range(3, ROW_BITS):
            stride = jnp.where(middle == r, WIDTH, jnp.left_shift(1, r - after_middle[r]))
            offsets += [offset + stride for offset in offsets]
    else:
        index = lax.broadcasted_iota(jnp.int32, (1, 2 * WIDTH), 1)
        rows = one_hot(2 * WIDTH, moved_bits(index, row_before, range(ROW_BITS)))
    old_lane = moved_bits(lane, range(LANE_BITS), lane_before)
    fetches[1].wait()
    fetches[2].wait()
    real, imag = halves(gates_ref[0, 0]), halves(gates_ref[0, 1])
    if folded:
        both = [dot(rows, jnp.concatenate([real[i], imag[i]], axis=1)).astype(BF16) for i in range(2)]
        real, imag = [[half[:, c * WIDTH : (c + 1) * WIDTH] for half in both] for c in range(2)]
    matrix0 = [block_matrix(real[i], imag[i]) for i in range(2)]
    real, imag = halves(gates_ref[1, 0]), halves(gates_ref[1, 1])
    matrix1 = [block_matrix(real[i], imag[i]) for i in range(2)]
    pieces = [[x_ref[pl.ds(m * 2 + c, WIDTH, stride=4), :] for m in range(2)] for c in range(2)]
    state = jnp.concatenate([jnp.concatenate(row, axis=1) for row in pieces], axis=0)
    state = dot3(matrix0, halves(state))
    if folded:
        for c in range(2):
            for m in range(2):
                work[c, m * WIDTH : (m + 1) * WIDTH] = state[c * WIDTH : (c + 1) * WIDTH, m * WIDTH : (m + 1) * WIDTH]
        state = halves(
            jnp.concatenate(
                [
                    jnp.concatenate([work[c, pl.ds(pl.multiple_of(offset, 8), 8), :] for offset in offsets], axis=0)
                    for c in range(2)
                ],
                axis=1,
            )
        )
    else:
        state = [dot(rows, half).astype(BF16) for half in halves(turned(state))]
    state = dot3(state, matrix1, transposed=True)
    before, after = masks_of(lane, crosses[3:], wanted[3:]), masks_of(lane, crosses[3:], slots[3:])
    index = lanes_of(old_lane, crosses[3:], wanted[3:])
    for c in range(2):
        values = [state[8 * v : 8 * v + 8, c * WIDTH : (c + 1) * WIDTH] for v in range(32)]
        for v, value in enumerate(crossed(values, before, after, index)):
            work[c, pl.ds(8 * v, 8), :] = value
    masks = masks_of(lane, crosses[:3], slots[:3])
    index = [None] + lanes_of(lane, crosses[:3], slots[:3])[1:]
    for c in range(2):
        for group in range(4):
            places = [pl.ds(group * 64 + o, 8, stride=8) for o in range(8)]
            values = crossed([work[c, place, :] for place in places], masks, masks, index)
            for place, value in zip(places, values, strict=True):
                work[c, place, :] = value
    me = lax.axis_index("lo")
    count = 2 * WIDTH // parts
    near = outs[0].shape[0]
    for step in range(parts):
        out = outs[0].at[step] if step < near else outs[1 + step - near]
        source = pl.multiple_of(jnp.bitwise_xor(me, step) * count, 8)
        for c in range(2):
            out[c] = work[c, pl.ds(source, count), :]


def turned(value):
    return jnp.concatenate(
        [
            jnp.concatenate([value[i * WIDTH : (i + 1) * WIDTH, j * WIDTH : (j + 1) * WIDTH] for i in range(2)], axis=1)
            for j in range(2)
        ],
        axis=0,
    )


def mixed(coefs_ref, own, other):
    own_r, own_i, other_r, other_i = [jnp.concatenate([coefs_ref[i]] * (own.shape[-2] // 8), axis=0) for i in range(4)]
    return (
        own_r * own[0] - own_i * own[1] + (other_r * other[0] - other_i * other[1]),
        own_r * own[1] + own_i * own[0] + (other_r * other[1] + other_i * other[0]),
    )


def mix_kernel(coefs_ref, matrix_ref, own_ref, other_ref, *outs):
    values = [mixed(coefs_ref, own_ref.at[k + 1], other_ref.at[k + 1]) for k in range(len(outs))]
    for out_ref, value in zip(outs, low_gate(matrix_ref, values), strict=True):
        out_ref[0], out_ref[1] = value


def arrival(parts):
    near = parts // 2
    return [0, *range(near, parts - 1)], [*range(1, near), parts - 1]


def low_weights_kernel(orders_ref, gate_hbm, gates_hbm, out_ref, coefs_out, mats_ref, gate_ref, sems):
    fetches = [
        pltpu.make_async_copy(gates_hbm.at[3], mats_ref, sems.at[0]),
        pltpu.make_async_copy(gate_hbm, gate_ref, sems.at[1]),
    ]
    for fetch in fetches:
        fetch.start()
    lanes = one_hot(WIDTH, orders_ref[0, 0:1])
    for fetch in fetches:
        fetch.wait()
    side = jnp.right_shift(lax.axis_index("hi"), lax.axis_size("hi").bit_length() - 2) & 1
    for other in range(2):
        for c in range(2):
            coefs_out[2 * other + c] = jnp.full((8, WIDTH), gate_ref[c, side, side ^ other])
    for i in range(2):
        real, imag = [dot(halves(mats_ref[c])[i], lanes).T for c in range(2)]
        out_ref[i] = block_matrix(real, -imag).astype(BF16)


def high_weights_kernel(lo_bits, orders_ref, gates_ref, early_ref, late_ref):
    parts = 1 << lo_bits
    kept = WIDTH // parts
    me = lax.axis_index("lo")
    index = lax.broadcasted_iota(jnp.int32, (1, WIDTH), 1)
    source = orders_ref[1, 0:1] % kept
    early, late = arrival(parts)
    for place, step in enumerate(early + late):
        source = source + jnp.where(index // kept == place, jnp.bitwise_xor(me, step) * kept, 0)
    rows = one_hot(WIDTH, source)

    def exact(left, right):
        return lax.dot_general(
            left, right, (((1,), (0,)), ((), ())), precision=lax.Precision.HIGHEST, preferred_element_type=F32
        )

    first, last = [[gates_ref[g, c] for c in range(2)] for g in (2, 4)]
    real = halves(exact(last[0], first[0]) - exact(last[1], first[1]))
    imag = halves(exact(last[0], first[1]) + exact(last[1], first[0]))
    half = len(early) * kept
    for i in range(2):
        both = [dot(part[i], rows) for part in (real, imag)]
        early_ref[i] = block_matrix(*[part[:, :half] for part in both]).astype(BF16)
        late_ref[i] = block_matrix(*[part[:, half:] for part in both]).astype(BF16)


def low_gate(matrix_ref, values):
    state = jnp.concatenate([jnp.concatenate(value, axis=1) for value in values], axis=0)
    state = dot3(halves(state), (matrix_ref[0], matrix_ref[1]))
    count = state.shape[0] // len(values)
    return [
        [state[i * count : (i + 1) * count, c * WIDTH : (c + 1) * WIDTH] for c in range(2)] for i in range(len(values))
    ]


def for_high(values):
    kept = values[0][0].shape[0] // 2
    return jnp.concatenate(
        [
            jnp.concatenate([value[c][m * kept : (m + 1) * kept] for m in range(2)], axis=1)
            for c in range(2)
            for value in values
        ],
        axis=0,
    )


def copy_kernel(in_ref, out_ref):
    out_ref[...] = in_ref[...]


def low_kernel(matrix_ref, in_ref, out_ref):
    (value,) = low_gate(matrix_ref, [(in_ref[0], in_ref[1])])
    out_ref[0], out_ref[1] = value


def early_kernel(coefs_ref, low_gate_ref, high_gate_ref, near_own_ref, near_other_ref, *refs):
    ins, out_ref = refs[:-1], refs[-1]
    values = [mixed(coefs_ref, near_own_ref.at[0], near_other_ref.at[0])]
    values += [mixed(coefs_ref, own, other) for own, other in zip(ins[0::2], ins[1::2], strict=True)]
    out_ref[...] = dot3((high_gate_ref[0], high_gate_ref[1]), halves(for_high(low_gate(low_gate_ref, values))))


def last_kernel(coefs_ref, high_gate_ref, early_ref, own_ref, other_ref, *refs):
    ins, (out_hbm, out_ref, sems) = refs[:-3], refs[-3:]
    values = [(ref[0], ref[1]) for ref in ins] + [mixed(coefs_ref, own_ref, other_ref)]
    high, low = halves(for_high(values))
    state = jnp.concatenate([low, high, high], axis=0)
    sends = []
    half = WIDTH // 4
    for i in range(4):
        matrix = [
            jnp.concatenate(
                [high_gate_ref[j, c * WIDTH + i * half : c * WIDTH + (i + 1) * half] for c in range(2)], axis=0
            )
            for j in (0, 1, 0)
        ]
        result = dot(jnp.concatenate(matrix, axis=1), state)
        for c in range(2):
            for m in range(2):
                at = c * WIDTH + i * half
                out_ref[pl.ds(i * 128 + m * 2 + c, half, stride=4), :] = (
                    early_ref[at : at + half, m * WIDTH : (m + 1) * WIDTH]
                    + result[c * half : (c + 1) * half, m * WIDTH : (m + 1) * WIDTH]
                )
        sends.append(
            pltpu.make_async_copy(out_ref.at[pl.ds(i * 128, 128)], out_hbm.at[pl.ds(i * 128, 128)], sems.at[i])
        )
        sends[-1].start()
    for send in sends:
        send.wait()


def swapped(block, axis, distance):
    count = lax.axis_size(axis)
    return lax.ppermute(block, axis, [(i, i ^ distance) for i in range(count)])


PARAMS = pltpu.CompilerParams(vmem_limit_bytes=8 << 20)
HBM = pl.BlockSpec(memory_space=pltpu.HBM)
VMEM = pl.BlockSpec(memory_space=pltpu.VMEM)


def in_hbm(value):
    return pltpu.with_memory_space_constraint(value, pltpu.HBM)


def on_device(amplitudes, gate_mats, dev_gate, qubit_order):
    parts = lax.axis_size("lo")
    lo_bits = parts.bit_length() - 1
    top = lax.axis_size("hi") // 2
    kept = WIDTH // parts
    rows = amplitudes.reshape(2, 256, WIDTH).transpose(1, 0, 2).reshape(512, WIDTH)
    block = pltpu.VMEM((2, 2 * kept, WIDTH), F32)
    near = parts // 2
    near_own, *far_own, orders = pl.pallas_call(
        functools.partial(first_kernel, lo_bits),
        out_shape=[pltpu.VMEM((near, 2, 2 * kept, WIDTH), F32)]
        + [block] * (parts - near)
        + [pltpu.VMEM((2, 8, WIDTH), jnp.int32)],
        in_specs=[HBM] * 3,
        out_specs=[VMEM] * (parts - near + 2),
        scratch_shapes=[
            pltpu.SMEM((LANE_BITS + ROW_BITS,), jnp.int32),
            pltpu.VMEM((512, WIDTH), F32),
            pltpu.VMEM((2, 2, WIDTH, WIDTH), F32),
            pltpu.VMEM((2, 256, WIDTH), F32),
            pltpu.SemaphoreType.DMA((3,)),
        ],
        compiler_params=PARAMS,
        name="first_gates",
    )(in_hbm(qubit_order), in_hbm(rows), in_hbm(gate_mats))
    near_other = swapped(near_own, "hi", top)
    far_own = [swapped(far, "lo", near + i) for i, far in enumerate(far_own)]
    counts = [2 * kept * len(steps) for steps in arrival(parts)]
    low_weights, coefs = pl.pallas_call(
        low_weights_kernel,
        out_shape=[pltpu.VMEM((2, 256, 256), BF16), pltpu.VMEM((4, 8, WIDTH), F32)],
        in_specs=[VMEM, HBM, HBM],
        out_specs=[VMEM] * 2,
        scratch_shapes=[pltpu.VMEM((2, WIDTH, WIDTH), F32), pltpu.SMEM((2, 2, 2), F32), pltpu.SemaphoreType.DMA((2,))],
        compiler_params=PARAMS,
        name="low_weights",
    )(orders, in_hbm(dev_gate), in_hbm(gate_mats))
    early_weights, late_weights = pl.pallas_call(
        functools.partial(high_weights_kernel, lo_bits),
        out_shape=[pltpu.VMEM((2, 256, count), BF16) for count in counts],
        in_specs=[VMEM, VMEM],
        out_specs=[VMEM] * 2,
        compiler_params=PARAMS,
        name="high_weights",
    )(orders, gate_mats)
    far_own[-1] = pl.pallas_call(
        low_kernel, out_shape=block, in_specs=[VMEM] * 2, out_specs=VMEM, compiler_params=PARAMS, name="low_gate"
    )(low_weights, far_own[-1])
    far_other = [swapped(far, "hi", top) for far in far_own]
    far_other[0] = pl.pallas_call(
        copy_kernel, out_shape=block, in_specs=[VMEM], out_specs=VMEM, compiler_params=PARAMS, name="arrived"
    )(far_other[0])
    mixes = pl.pallas_call(
        mix_kernel,
        out_shape=[block] * (near - 1),
        in_specs=[VMEM] * 4,
        out_specs=[VMEM] * (near - 1),
        compiler_params=PARAMS,
        name="mix_pair",
    )(coefs, low_weights, near_own, near_other)
    mixes = [swapped(mix, "lo", 1 + i) for i, mix in enumerate(mixes)]
    pairs = [value for pair in zip(far_own[:-1], far_other[:-1], strict=True) for value in pair]
    early = pl.pallas_call(
        early_kernel,
        out_shape=pltpu.VMEM((256, 256), F32),
        in_specs=[VMEM] * (5 + len(pairs)),
        out_specs=VMEM,
        compiler_params=PARAMS,
        name="early_gate",
    )(coefs, low_weights, early_weights, near_own, near_other, *pairs)
    out = pl.pallas_call(
        last_kernel,
        out_shape=jax.ShapeDtypeStruct((512, WIDTH), F32),
        in_specs=[VMEM] * (5 + len(mixes)),
        out_specs=HBM,
        scratch_shapes=[pltpu.VMEM((512, WIDTH), F32), pltpu.SemaphoreType.DMA((4,))],
        compiler_params=PARAMS,
        name="last_gates",
    )(coefs, late_weights, early, far_own[-1], far_other[-1], *mixes)
    return out.reshape(256, 2, WIDTH).transpose(1, 0, 2).reshape(2, -1)


def solution(mesh):
    return jax.shard_map(
        on_device,
        mesh=mesh,
        in_specs=(P(None, ("hi", "lo")), P(), P(), P()),
        out_specs=P(None, ("hi", "lo")),
        check_vma=False,
    )
```
